512 devices in a mesh: band: 64 (over x, z_lo, core), kpt: 8 (over z_hi, y).
Axes of the slice: x: 4, y: 4, z: 16 (z_hi: 2, z_lo: 8; z = z_hi * 8 + z_lo), core: 2. Of those that a mesh axis runs over, the one named last changes fastest.
Arguments:
- orbitals: bfloat16 [8, 128, 2, 48, 2304], P('kpt', 'band'), may hold values from -6 to 6
- kpoint_offsets: int32 [8, 3], replicated, may hold values from 0 to 1
- umklapp: int32 [8, 2, 3], P('kpt'), may hold values from -1 to 1
Outputs:
- exchange_applied: bfloat16 [8, 128, 2, 48, 2304], P('kpt', 'band')
The draws below stay inside these ranges and needn't reach their ends.
All inputs are finite; a program needn't handle non-finite values.
Results may differ from the reference program's by a relative error of at most 0.023.
Values may be sent and summed in bfloat16 or wider, within the bound.
A program may use at most 128 MiB of HBM per device.

```python
import math
import jax
import jax.numpy as jnp
from jax import lax

GRID = 48
BANDS_DEV = 2
SRC = 2
KSTEPS = 2
NB = 128
NK = 8
N_BAND = 64


def touch_ends(result, rng, smallest, high):
    shape = result.shape
    spot = [jax.random.randint(jax.random.fold_in(rng, axis), (), 0, shape[axis]) for axis in range(len(shape))]
    result = result.at[tuple(spot)].set(smallest)
    longest = shape.index(max(shape))
    spot[longest] = (spot[longest] + 1) % shape[longest]
    return result.at[tuple(spot)].set(high)


def level_of(key, shape, cuts, least, largest):
    gain, own = 1.0, jax.random.fold_in(key, 6)
    for axis_at, blocks in cuts:
        heights = jnp.exp(jax.random.uniform(jax.random.fold_in(own, axis_at), (blocks,), jnp.float32, least / len(cuts), largest / len(cuts)))
        gain = gain * jnp.repeat(heights, shape[axis_at] // blocks).reshape([-1 if axis == axis_at else 1 for axis in range(len(shape))])
    return gain


def normal_values(own_key, dims, scale, reach, cuts=(), kind=jnp.bfloat16):
    loudness = level_of(own_key, dims, cuts, -0.22, 0.18) if cuts else 1.0
    array = jax.random.normal(own_key, dims, jnp.float32) * scale * loudness
    return jnp.minimum(jnp.maximum(array, -reach), reach).astype(kind)


def setup_inputs(seed: int = 0) -> dict:
    splits = jax.random.split(jax.random.key(seed), 4)
    return {
        "orbitals": normal_values(splits[0], (NK, NB, 2, GRID, GRID * GRID), 1.0, 6.0, ((0, 8), (1, 64))),
        "kpoint_offsets": touch_ends(jax.random.randint(splits[1], (NK, 3), 0, 2), jax.random.fold_in(splits[1], 1), 0, 1).astype(jnp.int32),
        "umklapp": touch_ends(jax.random.randint(splits[2], (NK, KSTEPS, 3), -1, 2), jax.random.fold_in(splits[2], 1), -1, 1).astype(jnp.int32),
    }


def dft_tables(count):
    idx = jnp.arange(count, dtype=jnp.int32)
    phase = (idx[:, None] * idx[None, :] % count).astype(jnp.float32) * (2.0 * math.pi / count)
    scale = 1.0 / math.sqrt(count)
    return ((jnp.cos(phase) * scale).astype(jnp.bfloat16), (jnp.sin(phase) * scale).astype(jnp.bfloat16))

def one_axis(form, table, values):
    return jnp.einsum(form, table.astype(jnp.float32), values.astype(jnp.float32))

def transform(real_part, imag_part, cos_tab, sin_tab, inverse):
    sign = 1.0 if inverse else -1.0
    for form in ('ax,pxyz->payz', 'ay,pxyz->pxaz', 'az,pxyz->pxya'):
        cr = one_axis(form, cos_tab, real_part)
        ci = one_axis(form, cos_tab, imag_part)
        sr = one_axis(form, sin_tab, real_part)
        si = one_axis(form, sin_tab, imag_part)
        real_part = (cr - sign * si).astype(jnp.bfloat16)
        imag_part = (ci + sign * sr).astype(jnp.bfloat16)
    return (real_part, imag_part)

def screening(qvec, count):
    freq = ((jnp.arange(count, dtype=jnp.int32) + count // 2) % count - count // 2).astype(jnp.float32)
    kx = (freq + qvec[0]) ** 2
    ky = (freq + qvec[1]) ** 2
    kz = (freq + qvec[2]) ** 2
    return 4.0 / (kx[:, None, None] + ky[None, :, None] + kz[None, None, :] + 0.5)

def apply_block(targets, sources, kernel, cos_tab, sin_tab):
    count = cos_tab.shape[0]
    batch = targets.shape[0]
    t_re = targets[:, 0].reshape(batch, count, count, count).astype(jnp.float32)
    t_im = targets[:, 1].reshape(batch, count, count, count).astype(jnp.float32)
    acc_re = jnp.zeros((batch, count, count, count), jnp.float32)
    acc_im = jnp.zeros((batch, count, count, count), jnp.float32)
    for member in range(sources.shape[0]):
        m_re = sources[member, 0].reshape(count, count, count).astype(jnp.float32)
        m_im = sources[member, 1].reshape(count, count, count).astype(jnp.float32)
        d_re = (m_re * t_re + m_im * t_im).astype(jnp.bfloat16)
        d_im = (m_re * t_im - m_im * t_re).astype(jnp.bfloat16)
        f_re, f_im = transform(d_re, d_im, cos_tab, sin_tab, False)
        s_re = (f_re.astype(jnp.float32) * kernel).astype(jnp.bfloat16)
        s_im = (f_im.astype(jnp.float32) * kernel).astype(jnp.bfloat16)
        v_re, v_im = transform(s_re, s_im, cos_tab, sin_tab, True)
        v_re = v_re.astype(jnp.float32)
        v_im = v_im.astype(jnp.float32)
        acc_re = acc_re + (m_re * v_re - m_im * v_im)
        acc_im = acc_im + (m_re * v_im + m_im * v_re)
    return (acc_re, acc_im)

def reference(orbitals, kpoint_offsets, umklapp):
    count = GRID
    cos_tab, sin_tab = dft_tables(count)
    owner = N_BAND // 2 * BANDS_DEV
    results = []
    for kidx in range(NK):
        blocks = orbitals[kidx].reshape(NB // BANDS_DEV, BANDS_DEV, 2, count, count * count)
        total_re = jnp.zeros((NB // BANDS_DEV, BANDS_DEV, count, count, count), jnp.float32)
        total_im = jnp.zeros((NB // BANDS_DEV, BANDS_DEV, count, count, count), jnp.float32)
        for step in range(KSTEPS):
            other = (kidx - step) % NK
            sources = orbitals[other, owner:owner + SRC]
            qvec = 0.5 * (kpoint_offsets[kidx] - kpoint_offsets[other]).astype(jnp.float32) + umklapp[kidx, step].astype(jnp.float32)
            kernel = screening(qvec, count)
            part_re, part_im = lax.map(lambda tgt: apply_block(tgt, sources, kernel, cos_tab, sin_tab), blocks)
            total_re = total_re + part_re
            total_im = total_im + part_im
        merged = jnp.stack([-total_re, -total_im], axis=2).reshape(NB, 2, count, count * count)
        results.append(merged.astype(jnp.bfloat16))
    return jnp.stack(results, axis=0)
```

```python
import math

import jax
import jax.numpy as jnp
import numpy as np
from jax import lax
from jax.experimental import pallas as pl
from jax.experimental.pallas import tpu as pltpu
from jax.sharding import PartitionSpec as P

MESH = pl.DeviceIdType.MESH
KSTEPS = 2
RELAYS = (1, 4, 6)
HALF = 1152

G = 48
L = 128


def tables():
    idx = np.arange(G)
    ph = (idx[:, None] * idx[None, :] % G).astype(np.float32) * np.float32(2.0 * math.pi / G)
    scale = np.float32(1.0 / math.sqrt(G))
    c = (np.cos(ph) * scale).astype(np.float32)
    s = (np.sin(ph) * scale).astype(np.float32)
    right, left = [], []
    for sign in (1.0, -1.0):
        left.append(np.block([[c, sign * s], [-sign * s, c]]))
        big = np.zeros((256, 256), np.float32)
        for p in range(2):
            a = slice(p * G, p * G + G)
            b = slice(L + p * G, L + p * G + G)
            big[a, a] = c
            big[b, b] = c
            big[b, a] = sign * s
            big[a, b] = -sign * s
        right.append(big)
    return np.stack(left).astype(jnp.bfloat16), np.stack(right).astype(jnp.bfloat16)


def dot(a, b):
    return jnp.dot(a, b, preferred_element_type=jnp.float32)


def lanes():
    return lax.broadcasted_iota(jnp.int32, (G, L), 1)


def roll(v, s):
    s = s % L
    return v if s == 0 else pltpu.roll(v, s, 1)


def piece(tiles, j):
    o, t = (G * j) % L, (G * j) // L
    v = tiles[t]
    if o + G > L:
        v = jnp.where(lanes() >= o, v, tiles[t + 1])
    return v, o


def spread(tiles_a, tiles_b, j):
    a, o = piece(tiles_a, j)
    b, _ = piece(tiles_b, j)
    return jnp.where(lanes() < G, roll(a, -o), roll(b, G - o))


def load_tiles(ref, g, dt):
    base = g * 384 if isinstance(g, int) else pl.multiple_of(g * 384, 128)
    v = ref[:, pl.ds(base, 384)].astype(dt)
    return [v[:, i * L:(i + 1) * L] for i in range(3)]


def rows(i):
    if isinstance(i, int):
        return pl.ds(i * G, G)
    return pl.ds(pl.multiple_of(i * G, 16), G)


def relayout_targets(loc, tgt, dt):
    def body(g, _):
        for c in range(2):
            ta = load_tiles(loc.at[0, c], g, dt)
            tb = load_tiles(loc.at[1, c], g, dt)
            for j in range(8):
                tgt[c, rows(g * 8 + j), :] = spread(ta, tb, j).astype(jnp.bfloat16)
        return 0
    lax.fori_loop(0, 6, body, 0)


def make_kern(kern, s, q):
    def f(n):
        return ((n + G // 2) % G - G // 2).astype(jnp.float32)
    ly = lax.broadcasted_iota(jnp.int32, (G, L), 0)
    lz = lanes() % G
    yz = (f(ly) + q[1]) ** 2 + (f(lz) + q[2]) ** 2
    def body(x, _):
        kx = (f(x) + q[0]) ** 2
        kern[s, rows(x), :] = -4.0 / (kx + yz + 0.5)
        return 0
    lax.fori_loop(0, G, body, 0)


def pair_rhs(re0, re1, im0, im1):
    return jnp.concatenate(
        [jnp.concatenate([re0, re1], 1), jnp.concatenate([im0, im1], 1)], 0)


def phase_a(src, tgt, spr, b, left, right):
    bf = jnp.bfloat16
    rhs = []
    for g in range(6):
        tl = [load_tiles(src.at[c], g, bf) for c in range(2)]
        d = []
        for i in range(8):
            r = rows(g * 8 + i)
            m = [spread(tl[c], tl[c], i) for c in range(2)]
            spr[0, r, :] = m[0]
            spr[1, r, :] = m[1]
            mr, mi = m[0].astype(jnp.float32), m[1].astype(jnp.float32)
            tr, ti = tgt[0, r, :].astype(jnp.float32), tgt[1, r, :].astype(jnp.float32)
            d.append(jnp.concatenate([(mr * tr + mi * ti).astype(bf), (mr * ti - mi * tr).astype(bf)], 1))
        rhs.append(jnp.concatenate(d, 0))
    z = dot(jnp.concatenate(rhs, 0), right[0]).astype(bf)
    for y in range(0, G, 2):
        w = z[y * G:(y + 2) * G]
        o = dot(left[0], pair_rhs(w[:G, :L], w[G:, :L], w[:G, L:], w[G:, L:]))
        for i in range(2):
            for c in range(2):
                b[c, pl.ds(y + i, G, stride=G), :] = o[c * G:(c + 1) * G, i * L:(i + 1) * L]


def phase_b(b, cc, kern, left):
    bf = jnp.bfloat16
    for x in range(0, G, 2):
        v = [[b[c, rows(x + i), :].astype(bf) for i in range(2)] for c in range(2)]
        o = dot(left[0], pair_rhs(v[0][0], v[0][1], v[1][0], v[1][1]))
        k = jnp.concatenate([kern[rows(x), :], kern[rows(x + 1), :]], 1)
        o = dot(left[1], (o * jnp.concatenate([k, k], 0)).astype(bf))
        for i in range(2):
            for c in range(2):
                cc[c, pl.ds(x + i, G, stride=G), :] = o[c * G:(c + 1) * G, i * L:(i + 1) * L]


def phase_c(cc, spr, acc, left, right):
    bf = jnp.bfloat16
    n = 16
    def along_x(k):
        lhs = []
        for y in range(k * n, k * n + n, 2):
            v = [[cc[c, rows(y + i), :].astype(bf) for i in range(2)] for c in range(2)]
            o = dot(left[1], pair_rhs(v[0][0], v[0][1], v[1][0], v[1][1])).astype(bf)
            lhs += [jnp.concatenate([o[:G, :L], o[G:, :L]], 1), jnp.concatenate([o[:G, L:], o[G:, L:]], 1)]
        return jnp.concatenate(lhs, 0)
    lhs = along_x(0)
    for k in range(G // n):
        later = along_x(k + 1) if k + 1 < G // n else None
        p = dot(lhs, right[1])
        r = pl.ds(k * n * G, n * G)
        vr, vi = p[:, :L], p[:, L:]
        mr, mi = spr[0, r, :].astype(jnp.float32), spr[1, r, :].astype(jnp.float32)
        acc[0, r, :] += mr * vr - mi * vi
        acc[1, r, :] += mr * vi + mi * vr
        lhs = later


def gather_out(acc, out, dt):
    def body(g, _):
        ln = lanes()
        for c in range(2):
            a = [acc[c, rows(g * 8 + j), :].astype(dt) for j in range(8)]
            for p in range(2):
                tiles = [None] * 3
                for j in range(8):
                    o, t = (G * j) % L, (G * j) // L
                    r = roll(a[j], o - G * p)
                    tiles[t] = r if tiles[t] is None else jnp.where(ln >= o, r, tiles[t])
                    if o + G > L:
                        tiles[t + 1] = r
                base = pl.multiple_of(g * 384, 128)
                for t in range(3):
                    out[p, c, :, pl.ds(base + t * L, L)] = tiles[t].astype(jnp.bfloat16)
        return 0
    lax.fori_loop(0, 6, body, 0)


def share(loc, out, send, pieces, across, twin, sends):
    band, kpt = lax.axis_index("band"), lax.axis_index("kpt")
    nk = lax.axis_size("kpt")
    x, zl, core = band // 16, (band // 2) % 8, band % 2
    after, before = lax.rem(kpt + 1, nk), lax.rem(kpt + nk - 1, nk)
    root = 32
    is_root = band == root

    def at(bx, bz, bc):
        return bx * 16 + bz * 2 + bc

    def sites(ref, s, q, c, r):
        return ref.at[s, q // 2, c, pl.ds(r * 16, 16), pl.ds(pl.multiple_of((q % 2) * HALF, 128), HALF)]

    def xat(d):
        return lax.rem(x + d, 4)

    def scatter(s, q, r, c):
        return pltpu.make_async_remote_copy(
            src_ref=loc.at[q // 2, c, pl.ds(r * 16, 16), pl.ds((q % 2) * HALF, HALF)],
            dst_ref=sites(out, s, q, c, r),
            send_sem=send.at[s, q, r, c], recv_sem=pieces.at[s, r],
            device_id={"band": at(q, RELAYS[r], c), "kpt": kpt if s == 0 else after}, device_id_type=MESH)

    def column(s, r, d):
        return pltpu.make_async_remote_copy(
            src_ref=sites(out, s, x, core, r), dst_ref=sites(out, s, x, core, r),
            send_sem=sends.at[s, d - 1], recv_sem=pieces.at[s, r],
            device_id={"band": at(x, lax.rem(zl + d, 8), core), "kpt": kpt}, device_id_type=MESH)

    def row(s, r, d):
        return pltpu.make_async_remote_copy(
            src_ref=sites(out, s, x, core, r), dst_ref=sites(out, s, x, core, r),
            send_sem=sends.at[s, 7 + r * 3 + d - 1], recv_sem=across.at[s, r, d - 1],
            device_id={"band": at(xat(d), zl, core), "kpt": kpt}, device_id_type=MESH)

    def arrived(s, r, d):
        ref = sites(out, s, xat(4 - d), core, r)
        return pltpu.make_async_remote_copy(
            src_ref=ref, dst_ref=ref, send_sem=sends.at[s, 7 + r * 3 + d - 1], recv_sem=across.at[s, r, d - 1],
            device_id={"band": at(xat(d), zl, core), "kpt": kpt}, device_id_type=MESH)

    def to_twin(s, r, d, c):
        ref = sites(out, s, xat(4 - d) if d else x, c, r)
        return pltpu.make_async_remote_copy(
            src_ref=ref, dst_ref=ref, send_sem=sends.at[s, 16 + r * 4 + d], recv_sem=twin.at[s, r, d],
            device_id={"band": at(x, zl, 1 - core), "kpt": kpt}, device_id_type=MESH)

    relay = [zl == z for z in RELAYS]
    any_relay = relay[0] | relay[1] | relay[2]

    bar = pltpu.get_barrier_semaphore()

    def greet(b, k):
        pl.semaphore_signal(bar, inc=1, device_id={"band": b, "kpt": k}, device_id_type=MESH)

    @pl.when(any_relay)
    def _():
        greet(root, kpt)
        greet(root, before)

    for r in range(3):
        @pl.when(jnp.logical_not(relay[r]))
        def _():
            greet(at(x, RELAYS[r], core), kpt)
    for d in range(1, 4):
        greet(at(xat(d), zl, core), kpt)
    greet(at(x, zl, 1 - core), kpt)

    @pl.when(any_relay)
    def _():
        pl.semaphore_wait(bar, 11)

    @pl.when(jnp.logical_not(any_relay | is_root))
    def _():
        pl.semaphore_wait(bar, 4)

    @pl.when(is_root)
    def _():
        pl.semaphore_wait(bar, 52)
        for s in range(2):
            for r in range(3):
                for q in range(4):
                    for c in range(2):
                        scatter(s, q, r, c).start()

    def forward(s, r):
        column(s, r, 1).wait_recv()
        for d in range(1, 4):
            row(s, r, d).start()
        to_twin(s, r, 0, core).start()

    def lead(s):
        for r in range(3):
            @pl.when(relay[r])
            def _():
                column(s, r, 1).wait_recv()
                for d in range(1, 8):
                    column(s, r, d).start()
                for d in range(1, 4):
                    row(s, r, d).start()
                to_twin(s, r, 0, core).start()

    def rest(s):
        for r in range(3):
            @pl.when(jnp.logical_not(relay[r]))
            def _():
                forward(s, r)

    def take(s):
        for r in range(3):
            for d in (1, 3, 2):
                arrived(s, r, d).wait_recv()
                to_twin(s, r, d, core).start()

    def finish(s):
        for r in range(3):
            for d in range(4):
                to_twin(s, r, d, 1 - core).wait_recv()

    lead(0)
    rest(0)
    lead(1)
    take(0)
    rest(1)
    take(1)
    finish(0)
    finish(1)

    @pl.when(is_root)
    def _():
        for s in range(2):
            for r in range(3):
                for q in range(4):
                    for c in range(2):
                        scatter(s, q, r, c).wait_send()

    for s in range(2):
        @pl.when(any_relay)
        def _():
            for d in range(1, 8):
                column(s, 0, d).wait_send()
        for r in range(3):
            for d in range(1, 4):
                row(s, r, d).wait_send()
            for d in range(4):
                to_twin(s, r, d, core).wait_send()


def apply_all(koff, umk, loc, src, left, right, out, tgt, spr, b, cc, acc, kern):
    kpt = lax.axis_index("kpt")
    nk = lax.axis_size("kpt")
    relayout_targets(loc, tgt, jnp.bfloat16)
    for s in range(2):
        other = lax.rem(kpt + nk - s, nk)
        q = [0.5 * (koff[kpt, i] - koff[other, i]).astype(jnp.float32) + umk[s, i].astype(jnp.float32) for i in range(3)]
        make_kern(kern, s, q)
    acc[...] = jnp.zeros_like(acc)

    def one(u, _):
        phase_a(src.at[u // 2, u % 2], tgt, spr, b, left, right)
        phase_b(b, cc, kern.at[u // 2], left)
        phase_c(cc, spr, acc, left, right)
        return 0

    lax.fori_loop(0, 4, one, 0)
    gather_out(acc, out, jnp.float32)


def on_device(orbitals, koff, umklapp):
    bf = jnp.bfloat16
    loc = orbitals[0]
    left, right = tables()
    vmem = pl.BlockSpec(memory_space=pltpu.VMEM)
    smem = pl.BlockSpec(memory_space=pltpu.SMEM)
    src = pl.pallas_call(
        share,
        out_shape=jax.ShapeDtypeStruct((2,) + loc.shape, bf),
        in_specs=[vmem],
        out_specs=vmem,
        scratch_shapes=[
            pltpu.SemaphoreType.DMA((2, 4, 3, 2)),
            pltpu.SemaphoreType.DMA((2, 3)),
            pltpu.SemaphoreType.DMA((2, 3, 3)),
            pltpu.SemaphoreType.DMA((2, 3, 4)),
            pltpu.SemaphoreType.DMA((2, 28)),
        ],
        compiler_params=pltpu.CompilerParams(collective_id=0, has_side_effects=True, vmem_limit_bytes=32 * 2**20),
    )(loc)
    cube = (2, G * G, L)
    res = pl.pallas_call(
        apply_all,
        out_shape=jax.ShapeDtypeStruct(loc.shape, bf),
        in_specs=[smem, smem, vmem, vmem, vmem, vmem],
        out_specs=vmem,
        scratch_shapes=[pltpu.VMEM(cube, bf), pltpu.VMEM(cube, bf)] + [pltpu.VMEM(cube, jnp.float32)] * 4,
        compiler_params=pltpu.CompilerParams(vmem_limit_bytes=56 * 2**20),
    )(koff, umklapp[0], loc, src, jnp.asarray(left), jnp.asarray(right))
    return res[None]


def solution(mesh):
    return jax.shard_map(
        on_device,
        mesh=mesh,
        in_specs=(P("kpt", "band", None, None, None), P(), P("kpt", None, None)),
        out_specs=P("kpt", "band", None, None, None),
        check_vma=False,
    )
```

```python
import math

import jax
import jax.numpy as jnp
import numpy as np
from jax import lax
from jax.experimental import pallas as pl
from jax.experimental.pallas import tpu as pltpu
from jax.sharding import PartitionSpec as P

MESH = pl.DeviceIdType.MESH
KSTEPS = 2
RELAYS = (6, 4, 1)
HALF = 1152
ROOT = 32
SEEDS = ((2, 0), (3, 1)), ((1, 0), (0, 1))

G = 48
L = 128


def tables():
    idx = np.arange(G)
    ph = (idx[:, None] * idx[None, :] % G).astype(np.float32) * np.float32(2.0 * math.pi / G)
    scale = np.float32(1.0 / math.sqrt(G))
    c = (np.cos(ph) * scale).astype(np.float32)
    s = (np.sin(ph) * scale).astype(np.float32)
    right, left = [], []
    for sign in (1.0, -1.0):
        left.append(np.block([[c, sign * s], [-sign * s, c]]))
        big = np.zeros((256, 256), np.float32)
        for p in range(2):
            a = slice(p * G, p * G + G)
            b = slice(L + p * G, L + p * G + G)
            big[a, a] = c
            big[b, b] = c
            big[b, a] = sign * s
            big[a, b] = -sign * s
        right.append(big)
    return np.stack(left).astype(jnp.bfloat16), np.stack(right).astype(jnp.bfloat16)


def dot(a, b):
    return jnp.dot(a, b, preferred_element_type=jnp.float32)


def lanes():
    return lax.broadcasted_iota(jnp.int32, (G, L), 1)


def roll(v, s):
    s = s % L
    return v if s == 0 else pltpu.roll(v, s, 1)


def piece(tiles, j):
    o, t = (G * j) % L, (G * j) // L
    v = tiles[t]
    if o + G > L:
        v = jnp.where(lanes() >= o, v, tiles[t + 1])
    return v, o


def spread(tiles_a, tiles_b, j):
    a, o = piece(tiles_a, j)
    b, _ = piece(tiles_b, j)
    return jnp.where(lanes() < G, roll(a, -o), roll(b, G - o))


def load_tiles(ref, g, dt):
    base = g * 384 if isinstance(g, int) else pl.multiple_of(g * 384, 128)
    v = ref[:, pl.ds(base, 384)].astype(dt)
    return [v[:, i * L:(i + 1) * L] for i in range(3)]


def rows(i):
    if isinstance(i, int):
        return pl.ds(i * G, G)
    return pl.ds(pl.multiple_of(i * G, 16), G)


def relayout_targets(loc, tgt, dt):
    def body(g, _):
        for c in range(2):
            ta = load_tiles(loc.at[0, c], g, dt)
            tb = load_tiles(loc.at[1, c], g, dt)
            for j in range(8):
                tgt[c, rows(g * 8 + j), :] = spread(ta, tb, j).astype(jnp.bfloat16)
        return 0
    lax.fori_loop(0, 6, body, 0)


def make_kern(kern, s, q):
    def f(n):
        return ((n + G // 2) % G - G // 2).astype(jnp.float32)
    ly = lax.broadcasted_iota(jnp.int32, (G, L), 0)
    lz = lanes() % G
    yz = (f(ly) + q[1]) ** 2 + (f(lz) + q[2]) ** 2
    def body(x, _):
        kx = (f(x) + q[0]) ** 2
        kern[s, rows(x), :] = -4.0 / (kx + yz + 0.5)
        return 0
    lax.fori_loop(0, G, body, 0)


def pair_rhs(re0, re1, im0, im1):
    return jnp.concatenate(
        [jnp.concatenate([re0, re1], 1), jnp.concatenate([im0, im1], 1)], 0)


def phase_a(src, tgt, spr, b, left, right):
    bf = jnp.bfloat16
    rhs = []
    for g in range(6):
        tl = [load_tiles(src.at[c], g, bf) for c in range(2)]
        d = []
        for i in range(8):
            r = rows(g * 8 + i)
            m = [spread(tl[c], tl[c], i) for c in range(2)]
            spr[0, r, :] = m[0]
            spr[1, r, :] = m[1]
            mr, mi = m[0].astype(jnp.float32), m[1].astype(jnp.float32)
            tr, ti = tgt[0, r, :].astype(jnp.float32), tgt[1, r, :].astype(jnp.float32)
            d.append(jnp.concatenate([(mr * tr + mi * ti).astype(bf), (mr * ti - mi * tr).astype(bf)], 1))
        rhs.append(jnp.concatenate(d, 0))
    z = dot(jnp.concatenate(rhs, 0), right[0]).astype(bf)
    for y in range(0, G, 2):
        w = z[y * G:(y + 2) * G]
        o = dot(left[0], pair_rhs(w[:G, :L], w[G:, :L], w[:G, L:], w[G:, L:]))
        for i in range(2):
            for c in range(2):
                b[c, pl.ds(y + i, G, stride=G), :] = o[c * G:(c + 1) * G, i * L:(i + 1) * L]


def phase_b(b, cc, kern, left):
    bf = jnp.bfloat16
    for x in range(0, G, 2):
        v = [[b[c, rows(x + i), :].astype(bf) for i in range(2)] for c in range(2)]
        o = dot(left[0], pair_rhs(v[0][0], v[0][1], v[1][0], v[1][1]))
        k = jnp.concatenate([kern[rows(x), :], kern[rows(x + 1), :]], 1)
        o = dot(left[1], (o * jnp.concatenate([k, k], 0)).astype(bf))
        for i in range(2):
            for c in range(2):
                cc[c, pl.ds(x + i, G, stride=G), :] = o[c * G:(c + 1) * G, i * L:(i + 1) * L]


def phase_c(cc, spr, acc, left, right):
    bf = jnp.bfloat16
    n = 16
    def along_x(k):
        lhs = []
        for y in range(k * n, k * n + n, 2):
            v = [[cc[c, rows(y + i), :].astype(bf) for i in range(2)] for c in range(2)]
            o = dot(left[1], pair_rhs(v[0][0], v[0][1], v[1][0], v[1][1])).astype(bf)
            lhs += [jnp.concatenate([o[:G, :L], o[G:, :L]], 1), jnp.concatenate([o[:G, L:], o[G:, L:]], 1)]
        return jnp.concatenate(lhs, 0)
    lhs = along_x(0)
    for k in range(G // n):
        later = along_x(k + 1) if k + 1 < G // n else None
        p = dot(lhs, right[1])
        r = pl.ds(k * n * G, n * G)
        vr, vi = p[:, :L], p[:, L:]
        mr, mi = spr[0, r, :].astype(jnp.float32), spr[1, r, :].astype(jnp.float32)
        acc[0, r, :] += mr * vr - mi * vi
        acc[1, r, :] += mr * vi + mi * vr
        lhs = later


def gather_out(acc, out, dt):
    def body(g, _):
        ln = lanes()
        for c in range(2):
            a = [acc[c, rows(g * 8 + j), :].astype(dt) for j in range(8)]
            for p in range(2):
                tiles = [None] * 3
                for j in range(8):
                    o, t = (G * j) % L, (G * j) // L
                    r = roll(a[j], o - G * p)
                    tiles[t] = r if tiles[t] is None else jnp.where(ln >= o, r, tiles[t])
                    if o + G > L:
                        tiles[t + 1] = r
                base = pl.multiple_of(g * 384, 128)
                for t in range(3):
                    out[p, c, :, pl.ds(base + t * L, L)] = tiles[t].astype(jnp.bfloat16)
        return 0
    lax.fori_loop(0, 6, body, 0)


def kernel(loc, koff, umk, left_in, right_in, out, src, tgt, spr, b, cc, acc, kern, mine, left, right, held, ks, us,
           local, first, seeded, seed_send, pieces, across, twin, sends):
    band, kpt = lax.axis_index("band"), lax.axis_index("kpt")
    nk = lax.axis_size("kpt")
    x, zl, core = band // 16, (band // 2) % 8, band % 2
    after, before = lax.rem(kpt + 1, nk), lax.rem(kpt + nk - 1, nk)
    is_root = band == ROOT

    def at(bx, bz, bc):
        return bx * 16 + bz * 2 + bc

    def xat(d):
        return lax.rem(x + d, 4)

    def site(s, u, q, r):
        return src.at[s, u, q // 2, pl.ds(r * 16, 16), pl.ds(pl.multiple_of((q % 2) * HALF, 128), HALF)]

    def held_piece(q, r):
        return held.at[q // 2, pl.ds(r * 16, 16), pl.ds((q % 2) * HALF, HALF)]

    def remote(source, target, send, recv, b_, k_=kpt):
        return pltpu.make_async_remote_copy(
            src_ref=source, dst_ref=target, send_sem=send, recv_sem=recv,
            device_id={"band": b_, "kpt": k_}, device_id_type=MESH)

    def from_root(s, u, q, r):
        own = s == 0 and u == 0
        target = site(s, u, q, r) if own else held_piece(q, r)
        to = at(q, RELAYS[r], 0) if own else at(SEEDS[s][u][0], 0, u)
        return remote(
            loc.at[u, q // 2, pl.ds(r * 16, 16), pl.ds((q % 2) * HALF, HALF)], target,
            first.at[s * 2 + u, q, r], pieces.at[s, r] if own else seeded.at[q, r], to, kpt if s == 0 else after)

    def from_seed(s, u, q, r):
        return remote(held_piece(q, r), site(s, u, q, r), seed_send.at[q, r], pieces.at[s, r], at(q, RELAYS[r], u))

    def column(s, r, d):
        ref = site(s, core, x, r)
        return remote(ref, ref, sends.at[s, d - 1], pieces.at[s, r], at(x, lax.rem(zl + d, 8), core))

    def row(s, r, d):
        ref = site(s, core, x, r)
        return remote(ref, ref, sends.at[s, 7 + r * 3 + d - 1], across.at[s, r, d - 1], at(xat(d), zl, core))

    def arrived(s, r, d):
        ref = site(s, core, xat(4 - d), r)
        return remote(ref, ref, sends.at[s, 7 + r * 3 + d - 1], across.at[s, r, d - 1], at(xat(d), zl, core))

    def to_twin(s, r, d, u):
        ref = site(s, u, xat(4 - d) if d else x, r)
        return remote(ref, ref, sends.at[s, 16 + r * 4 + d], twin.at[s, r, d], at(x, zl, 1 - core))

    relay = [zl == z for z in RELAYS]
    any_relay = relay[0] | relay[1] | relay[2]
    seeds = [(s, u, (x == SEEDS[s][u][0]) & (zl == 0) & (core == u)) for s, u in ((0, 1), (1, 0), (1, 1))]
    any_seed = seeds[0][2] | seeds[1][2] | seeds[2][2]

    bar = pltpu.get_barrier_semaphore()

    def greet(b_, k_=kpt):
        pl.semaphore_signal(bar, inc=1, device_id={"band": b_, "kpt": k_}, device_id_type=MESH)

    @pl.when(any_relay)
    def _():
        for s in range(2):
            greet(jnp.where(core == 0, at(SEEDS[s][0][0], 0, 0), at(SEEDS[s][1][0], 0, 1)))

    for s, u, here in seeds:
        @pl.when(here)
        def _():
            greet(ROOT, kpt if s == 0 else before)

    for r in range(3):
        @pl.when(jnp.logical_not(relay[r]))
        def _():
            greet(at(x, RELAYS[r], core))
    for d in range(1, 4):
        greet(at(xat(d), zl, core))
    greet(at(x, zl, 1 - core))

    copies = [pltpu.make_async_copy(a, c, local.at[i]) for i, (a, c) in enumerate(
        ((loc, mine), (left_in, left), (right_in, right), (koff, ks), (umk, us)))]
    for c in copies:
        c.start()

    @pl.when(any_relay)
    def _():
        pl.semaphore_wait(bar, 11)

    @pl.when(any_seed)
    def _():
        pl.semaphore_wait(bar, 16)

    @pl.when(is_root)
    def _():
        pl.semaphore_wait(bar, 19)

    @pl.when(jnp.logical_not(any_relay | any_seed | is_root))
    def _():
        pl.semaphore_wait(bar, 4)

    def each_piece(f):
        for r in range(3):
            for q in range(4):
                f(q, r)

    @pl.when(is_root)
    def _():
        each_piece(lambda q, r: [from_root(s, u, q, r).start() for s, u in ((0, 0), (0, 1))])
        each_piece(lambda q, r: [from_root(s, u, q, r).start() for s, u in ((1, 0), (1, 1))])

    for c in copies:
        c.wait()
    relayout_targets(mine, tgt, jnp.bfloat16)
    for s in range(2):
        other = lax.rem(kpt + nk - s, nk)
        make_kern(kern, s, [0.5 * (ks[i, kpt] - ks[i, other]).astype(jnp.float32) + us[s, i].astype(jnp.float32) for i in range(3)])
    acc[...] = jnp.zeros_like(acc)

    for s, u, here in seeds:
        @pl.when(here)
        def _():
            def pass_on(q, r):
                from_root(s, u, q, r).wait_recv()
                from_seed(s, u, q, r).start()
            each_piece(pass_on)

    def spread_piece(s, r):
        for d in (2, 1, 3):
            row(s, r, d).start()
        to_twin(s, r, 0, core).start()

    def lead(s):
        for r in range(3):
            @pl.when(relay[r])
            def _():
                column(s, r, 1).wait_recv()
                for d in range(1, 8):
                    column(s, r, d).start()
                spread_piece(s, r)

    def rest(s):
        for r in range(3):
            @pl.when(jnp.logical_not(relay[r]))
            def _():
                column(s, r, 1).wait_recv()
                spread_piece(s, r)

    def take(s):
        for r in range(3):
            for d in (1, 3, 2):
                arrived(s, r, d).wait_recv()
                to_twin(s, r, d, core).start()

    def finish(s):
        for r in range(3):
            for d in range(4):
                to_twin(s, r, d, 1 - core).wait_recv()

    lead(0)
    rest(0)
    lead(1)
    take(0)

    def one(u, _):
        m = lax.rem(core + u, 2)

        @pl.when(u == 1)
        def _():
            finish(0)

        @pl.when(u == 3)
        def _():
            finish(1)

        phase_a(src.at[u // 2, m], tgt, spr, b, left, right)

        @pl.when(u == 0)
        def _():
            rest(1)

        phase_b(b, cc, kern.at[u // 2], left)

        @pl.when(u == 1)
        def _():
            take(1)

        phase_c(cc, spr, acc, left, right)
        return 0

    lax.fori_loop(0, 4, one, 0)
    gather_out(acc, out, jnp.float32)

    @pl.when(is_root)
    def _():
        each_piece(lambda q, r: [from_root(s, u, q, r).wait_send() for s in range(2) for u in range(2)])

    @pl.when(any_seed)
    def _():
        each_piece(lambda q, r: from_seed(0, 1, q, r).wait_send())

    for s in range(2):
        @pl.when(any_relay)
        def _():
            for d in range(1, 8):
                column(s, 0, d).wait_send()
        for r in range(3):
            for d in range(1, 4):
                row(s, r, d).wait_send()
            for d in range(4):
                to_twin(s, r, d, core).wait_send()


def on_device(orbitals, koff, umklapp):
    bf = jnp.bfloat16
    loc = orbitals[0]
    left, right = tables()
    hbm = pl.BlockSpec(memory_space=pl.ANY)
    dma = pltpu.SemaphoreType.DMA
    cube = (2, G * G, L)
    res = pl.pallas_call(
        kernel,
        out_shape=jax.ShapeDtypeStruct(loc.shape, bf),
        in_specs=[hbm] * 5,
        out_specs=pl.BlockSpec(memory_space=pltpu.VMEM),
        scratch_shapes=[pltpu.VMEM((2,) + loc.shape, bf), pltpu.VMEM(cube, bf), pltpu.VMEM(cube, bf)]
        + [pltpu.VMEM(cube, jnp.float32)] * 4
        + [pltpu.VMEM(loc.shape, bf), pltpu.VMEM(left.shape, bf), pltpu.VMEM(right.shape, bf), pltpu.VMEM(loc.shape[1:], bf)]
        + [pltpu.SMEM((3, koff.shape[0]), jnp.int32), pltpu.SMEM(umklapp.shape[1:], jnp.int32)]
        + [dma((5,)), dma((4, 4, 3)), dma((4, 3)), dma((4, 3)), dma((2, 3)), dma((2, 3, 3)), dma((2, 3, 4)), dma((2, 28))],
        compiler_params=pltpu.CompilerParams(collective_id=0, has_side_effects=True, vmem_limit_bytes=56 * 2**20),
    )(loc, koff.T, umklapp[0], jnp.asarray(left), jnp.asarray(right))
    return res[None]


def solution(mesh):
    return jax.shard_map(
        on_device,
        mesh=mesh,
        in_specs=(P("kpt", "band", None, None, None), P(), P("kpt", None, None)),
        out_specs=P("kpt", "band", None, None, None),
        check_vma=False,
    )
```

```python
import math

import jax
import jax.numpy as jnp
import numpy as np
from jax import lax
from jax.experimental import pallas as pl
from jax.experimental.pallas import tpu as pltpu
from jax.sharding import PartitionSpec as P

MESH = pl.DeviceIdType.MESH
KSTEPS = 2
RELAYS = (6, 4, 1)
HALF = 1152
ROOT = 32
SEEDS = ((2, 0), (3, 1)), ((1, 0), (0, 1))

G = 48
L = 128


def tables():
    idx = np.arange(G)
    ph = (idx[:, None] * idx[None, :] % G).astype(np.float32) * np.float32(2.0 * math.pi / G)
    scale = np.float32(1.0 / math.sqrt(G))
    c = (np.cos(ph) * scale).astype(np.float32)
    s = (np.sin(ph) * scale).astype(np.float32)
    right, left = [], []
    for sign in (1.0, -1.0):
        left.append(np.block([[c, sign * s], [-sign * s, c]]))
        big = np.zeros((256, 256), np.float32)
        for p in range(2):
            a = slice(p * G, p * G + G)
            b = slice(L + p * G, L + p * G + G)
            big[a, a] = c
            big[b, b] = c
            big[b, a] = sign * s
            big[a, b] = -sign * s
        right.append(big)
    return np.stack(left).astype(jnp.bfloat16), np.stack(right).astype(jnp.bfloat16)


def dot(a, b):
    return jnp.dot(a, b, preferred_element_type=jnp.float32)


def lanes():
    return lax.broadcasted_iota(jnp.int32, (G, L), 1)


def roll(v, s):
    s = s % L
    return v if s == 0 else pltpu.roll(v, s, 1)


def piece(tiles, j):
    o, t = (G * j) % L, (G * j) // L
    v = tiles[t]
    if o + G > L:
        v = jnp.where(lanes() >= o, v, tiles[t + 1])
    return v, o


def spread(tiles_a, tiles_b, j):
    a, o = piece(tiles_a, j)
    b, _ = piece(tiles_b, j)
    return jnp.where(lanes() < G, roll(a, -o), roll(b, G - o))


def load_tiles(ref, g, dt):
    base = g * 384 if isinstance(g, int) else pl.multiple_of(g * 384, 128)
    v = ref[:, pl.ds(base, 384)].astype(dt)
    return [v[:, i * L:(i + 1) * L] for i in range(3)]


def rows(i):
    if isinstance(i, int):
        return pl.ds(i * G, G)
    return pl.ds(pl.multiple_of(i * G, 16), G)


def relayout_targets(loc, tgt, dt):
    def body(g, _):
        for c in range(2):
            ta = load_tiles(loc.at[0, c], g, dt)
            tb = load_tiles(loc.at[1, c], g, dt)
            for j in range(8):
                tgt[c, rows(g * 8 + j), :] = spread(ta, tb, j).astype(jnp.bfloat16)
        return 0
    lax.fori_loop(0, 6, body, 0)


def make_kern(kern, s, q):
    def f(n):
        return ((n + G // 2) % G - G // 2).astype(jnp.float32)
    ly = lax.broadcasted_iota(jnp.int32, (G, L), 0)
    lz = lanes() % G
    yz = (f(ly) + q[1]) ** 2 + (f(lz) + q[2]) ** 2
    def body(x, _):
        kx = (f(x) + q[0]) ** 2
        kern[s, rows(x), :] = -4.0 / (kx + yz + 0.5)
        return 0
    lax.fori_loop(0, G, body, 0)


def pair_rhs(re0, re1, im0, im1):
    return jnp.concatenate(
        [jnp.concatenate([re0, re1], 1), jnp.concatenate([im0, im1], 1)], 0)


def phase_a(src, tgt, spr, b, left, right):
    bf = jnp.bfloat16
    rhs = []
    for g in range(6):
        tl = [load_tiles(src.at[c], g, bf) for c in range(2)]
        d = []
        for i in range(8):
            r = rows(g * 8 + i)
            m = [spread(tl[c], tl[c], i) for c in range(2)]
            spr[0, r, :] = m[0]
            spr[1, r, :] = m[1]
            mr, mi = m[0].astype(jnp.float32), m[1].astype(jnp.float32)
            tr, ti = tgt[0, r, :].astype(jnp.float32), tgt[1, r, :].astype(jnp.float32)
            d.append(jnp.concatenate([(mr * tr + mi * ti).astype(bf), (mr * ti - mi * tr).astype(bf)], 1))
        rhs.append(jnp.concatenate(d, 0))
    z = dot(jnp.concatenate(rhs, 0), right[0]).astype(bf)
    for y in range(0, G, 2):
        w = z[y * G:(y + 2) * G]
        o = dot(left[0], pair_rhs(w[:G, :L], w[G:, :L], w[:G, L:], w[G:, L:]))
        for i in range(2):
            for c in range(2):
                b[c, pl.ds(y + i, G, stride=G), :] = o[c * G:(c + 1) * G, i * L:(i + 1) * L]


def phase_b(b, cc, kern, left):
    bf = jnp.bfloat16
    for x in range(0, G, 2):
        v = [[b[c, rows(x + i), :].astype(bf) for i in range(2)] for c in range(2)]
        o = dot(left[0], pair_rhs(v[0][0], v[0][1], v[1][0], v[1][1]))
        k = jnp.concatenate([kern[rows(x), :], kern[rows(x + 1), :]], 1)
        o = dot(left[1], (o * jnp.concatenate([k, k], 0)).astype(bf))
        for i in range(2):
            for c in range(2):
                cc[c, pl.ds(x + i, G, stride=G), :] = o[c * G:(c + 1) * G, i * L:(i + 1) * L]


def phase_c(cc, spr, acc, left, right):
    bf = jnp.bfloat16
    n = 16
    def along_x(k):
        lhs = []
        for y in range(k * n, k * n + n, 2):
            v = [[cc[c, rows(y + i), :].astype(bf) for i in range(2)] for c in range(2)]
            o = dot(left[1], pair_rhs(v[0][0], v[0][1], v[1][0], v[1][1])).astype(bf)
            lhs += [jnp.concatenate([o[:G, :L], o[G:, :L]], 1), jnp.concatenate([o[:G, L:], o[G:, L:]], 1)]
        return jnp.concatenate(lhs, 0)
    lhs = along_x(0)
    for k in range(G // n):
        later = along_x(k + 1) if k + 1 < G // n else None
        p = dot(lhs, right[1])
        r = pl.ds(k * n * G, n * G)
        vr, vi = p[:, :L], p[:, L:]
        mr, mi = spr[0, r, :].astype(jnp.float32), spr[1, r, :].astype(jnp.float32)
        acc[0, r, :] += mr * vr - mi * vi
        acc[1, r, :] += mr * vi + mi * vr
        lhs = later


def gather_out(acc, out, dt):
    def body(g, _):
        ln = lanes()
        for c in range(2):
            a = [acc[c, rows(g * 8 + j), :].astype(dt) for j in range(8)]
            for p in range(2):
                tiles = [None] * 3
                for j in range(8):
                    o, t = (G * j) % L, (G * j) // L
                    r = roll(a[j], o - G * p)
                    tiles[t] = r if tiles[t] is None else jnp.where(ln >= o, r, tiles[t])
                    if o + G > L:
                        tiles[t + 1] = r
                base = pl.multiple_of(g * 384, 128)
                for t in range(3):
                    out[p, c, :, pl.ds(base + t * L, L)] = tiles[t].astype(jnp.bfloat16)
        return 0
    lax.fori_loop(0, 6, body, 0)


def kernel(loc, koff, umk, left_in, right_in, out, src, tgt, spr, b, cc, acc, kern, mine, left, right, held, ks, us,
           local, first, seeded, seed_send, pieces, across, twin, sends):
    band, kpt = lax.axis_index("band"), lax.axis_index("kpt")
    nk = lax.axis_size("kpt")
    x, zl, core = band // 16, (band // 2) % 8, band % 2
    after, before = lax.rem(kpt + 1, nk), lax.rem(kpt + nk - 1, nk)
    is_root = band == ROOT

    def at(bx, bz, bc):
        return bx * 16 + bz * 2 + bc

    def xat(d):
        return lax.rem(x + d, 4)

    def site(s, u, q, r):
        return src.at[s, u, q // 2, pl.ds(r * 16, 16), pl.ds(pl.multiple_of((q % 2) * HALF, 128), HALF)]

    def held_piece(q, r):
        return held.at[q // 2, pl.ds(r * 16, 16), pl.ds((q % 2) * HALF, HALF)]

    def remote(source, target, send, recv, b_, k_=kpt):
        return pltpu.make_async_remote_copy(
            src_ref=source, dst_ref=target, send_sem=send, recv_sem=recv,
            device_id={"band": b_, "kpt": k_}, device_id_type=MESH)

    def from_root(s, u, q, r):
        own = s == 0 and u == 0
        target = site(s, u, q, r) if own else held_piece(q, r)
        to = at(q, RELAYS[r], 0) if own else at(SEEDS[s][u][0], seed_z(s, after), u)
        return remote(
            loc.at[u, q // 2, pl.ds(r * 16, 16), pl.ds((q % 2) * HALF, HALF)], target,
            first.at[s * 2 + u, q, r], pieces.at[s, r] if own else seeded.at[q, r], to, kpt if s == 0 else after)

    def from_seed(s, u, q, r):
        return remote(held_piece(q, r), site(s, u, q, r), seed_send.at[q, r], pieces.at[s, r], at(q, RELAYS[r], u))

    def column(s, r, d):
        ref = site(s, core, x, r)
        return remote(ref, ref, sends.at[s, d - 1], pieces.at[s, r], at(x, lax.rem(zl + d, 8), core))

    def row(s, r, d):
        ref = site(s, core, x, r)
        return remote(ref, ref, sends.at[s, 7 + r * 3 + d - 1], across.at[s, r, d - 1], at(xat(d), zl, core))

    def arrived(s, r, d):
        ref = site(s, core, xat(4 - d), r)
        return remote(ref, ref, sends.at[s, 7 + r * 3 + d - 1], across.at[s, r, d - 1], at(xat(d), zl, core))

    def to_twin(s, r, d, u):
        ref = site(s, u, xat(4 - d) if d else x, r)
        return remote(ref, ref, sends.at[s, 16 + r * 4 + d], twin.at[s, r, d], at(x, zl, 1 - core))

    def seed_z(s, k):
        return jnp.where(lax.rem(k, 4) == 0, 7, 0) if s else 0

    relay = [zl == z for z in RELAYS]
    any_relay = relay[0] | relay[1] | relay[2]
    seeds = [(s, u, (x == SEEDS[s][u][0]) & (zl == seed_z(s, kpt)) & (core == u)) for s, u in ((0, 1), (1, 0), (1, 1))]
    any_seed = seeds[0][2] | seeds[1][2] | seeds[2][2]

    bar = pltpu.get_barrier_semaphore()

    def greet(b_, k_=kpt):
        pl.semaphore_signal(bar, inc=1, device_id={"band": b_, "kpt": k_}, device_id_type=MESH)

    @pl.when(any_relay)
    def _():
        for s in range(2):
            greet(jnp.where(core == 0, at(SEEDS[s][0][0], seed_z(s, kpt), 0), at(SEEDS[s][1][0], seed_z(s, kpt), 1)))

    for s, u, here in seeds:
        @pl.when(here)
        def _():
            greet(ROOT, kpt if s == 0 else before)

    for r in range(3):
        @pl.when(jnp.logical_not(relay[r]))
        def _():
            greet(at(x, RELAYS[r], core))
    for d in range(1, 4):
        greet(at(xat(d), zl, core))
    greet(at(x, zl, 1 - core))

    copies = [pltpu.make_async_copy(a, c, local.at[i]) for i, (a, c) in enumerate(
        ((loc, mine), (left_in, left), (right_in, right), (koff, ks), (umk, us)))]
    for c in copies:
        c.start()

    @pl.when(any_relay)
    def _():
        pl.semaphore_wait(bar, 11)

    @pl.when(any_seed)
    def _():
        pl.semaphore_wait(bar, 16)

    @pl.when(is_root)
    def _():
        pl.semaphore_wait(bar, 19)

    @pl.when(jnp.logical_not(any_relay | any_seed | is_root))
    def _():
        pl.semaphore_wait(bar, 4)

    def each_piece(f):
        for r in range(3):
            for q in range(4):
                f(q, r)

    @pl.when(is_root)
    def _():
        each_piece(lambda q, r: [from_root(s, u, q, r).start() for s, u in ((0, 0), (0, 1))])
        each_piece(lambda q, r: [from_root(s, u, q, r).start() for s, u in ((1, 0), (1, 1))])

    for c in copies:
        c.wait()
    relayout_targets(mine, tgt, jnp.bfloat16)
    for s in range(2):
        other = lax.rem(kpt + nk - s, nk)
        make_kern(kern, s, [0.5 * (ks[i, kpt] - ks[i, other]).astype(jnp.float32) + us[s, i].astype(jnp.float32) for i in range(3)])
    acc[...] = jnp.zeros_like(acc)

    for s, u, here in seeds:
        @pl.when(here)
        def _():
            def pass_on(q, r):
                from_root(s, u, q, r).wait_recv()
                from_seed(s, u, q, r).start()
            each_piece(pass_on)

    def spread_piece(s, r):
        for d in (2, 1, 3):
            row(s, r, d).start()
        to_twin(s, r, 0, core).start()

    def lead(s):
        for r in range(3):
            @pl.when(relay[r])
            def _():
                column(s, r, 1).wait_recv()
                for d in range(1, 8):
                    column(s, r, d).start()
                spread_piece(s, r)

    def rest(s):
        for r in range(3):
            @pl.when(jnp.logical_not(relay[r]))
            def _():
                column(s, r, 1).wait_recv()
                spread_piece(s, r)

    def take(s):
        for r in range(3):
            for d in (1, 3, 2):
                arrived(s, r, d).wait_recv()
                to_twin(s, r, d, core).start()

    def finish(s):
        for r in range(3):
            for d in range(4):
                to_twin(s, r, d, 1 - core).wait_recv()

    lead(0)
    rest(0)
    lead(1)
    take(0)

    def one(u, _):
        m = lax.rem(core + u, 2)

        @pl.when(u == 1)
        def _():
            finish(0)

        @pl.when(u == 3)
        def _():
            finish(1)

        phase_a(src.at[u // 2, m], tgt, spr, b, left, right)

        @pl.when(u == 0)
        def _():
            rest(1)

        phase_b(b, cc, kern.at[u // 2], left)

        @pl.when(u == 1)
        def _():
            take(1)

        phase_c(cc, spr, acc, left, right)
        return 0

    lax.fori_loop(0, 4, one, 0)
    gather_out(acc, out, jnp.float32)

    @pl.when(is_root)
    def _():
        each_piece(lambda q, r: [from_root(s, u, q, r).wait_send() for s in range(2) for u in range(2)])

    @pl.when(any_seed)
    def _():
        each_piece(lambda q, r: from_seed(0, 1, q, r).wait_send())

    for s in range(2):
        @pl.when(any_relay)
        def _():
            for d in range(1, 8):
                column(s, 0, d).wait_send()
        for r in range(3):
            for d in range(1, 4):
                row(s, r, d).wait_send()
            for d in range(4):
                to_twin(s, r, d, core).wait_send()


def on_device(orbitals, koff, umklapp):
    bf = jnp.bfloat16
    loc = orbitals[0]
    left, right = tables()
    hbm = pl.BlockSpec(memory_space=pl.ANY)
    dma = pltpu.SemaphoreType.DMA
    cube = (2, G * G, L)
    res = pl.pallas_call(
        kernel,
        out_shape=jax.ShapeDtypeStruct(loc.shape, bf),
        in_specs=[hbm] * 5,
        out_specs=pl.BlockSpec(memory_space=pltpu.VMEM),
        scratch_shapes=[pltpu.VMEM((2,) + loc.shape, bf), pltpu.VMEM(cube, bf), pltpu.VMEM(cube, bf)]
        + [pltpu.VMEM(cube, jnp.float32)] * 4
        + [pltpu.VMEM(loc.shape, bf), pltpu.VMEM(left.shape, bf), pltpu.VMEM(right.shape, bf), pltpu.VMEM(loc.shape[1:], bf)]
        + [pltpu.SMEM((3, koff.shape[0]), jnp.int32), pltpu.SMEM(umklapp.shape[1:], jnp.int32)]
        + [dma((5,)), dma((4, 4, 3)), dma((4, 3)), dma((4, 3)), dma((2, 3)), dma((2, 3, 3)), dma((2, 3, 4)), dma((2, 28))],
        compiler_params=pltpu.CompilerParams(collective_id=0, has_side_effects=True, vmem_limit_bytes=56 * 2**20),
    )(loc, koff.T, umklapp[0], jnp.asarray(left), jnp.asarray(right))
    return res[None]


def solution(mesh):
    return jax.shard_map(
        on_device,
        mesh=mesh,
        in_specs=(P("kpt", "band", None, None, None), P(), P("kpt", None, None)),
        out_specs=P("kpt", "band", None, None, None),
        check_vma=False,
    )
```

```python
import math

import jax
import jax.numpy as jnp
import numpy as np
from jax import lax
from jax.experimental import pallas as pl
from jax.experimental.pallas import tpu as pltpu
from jax.sharding import PartitionSpec as P

MESH = pl.DeviceIdType.MESH
KSTEPS = 2
RELAYS = (3, 2, 1)
HALF = 1152
ROOT = 32
SEEDS = ((2, 0), (3, 1)), ((1, 0), (0, 1))

G = 48
L = 128


def tables():
    idx = np.arange(G)
    ph = (idx[:, None] * idx[None, :] % G).astype(np.float32) * np.float32(2.0 * math.pi / G)
    scale = np.float32(1.0 / math.sqrt(G))
    c = (np.cos(ph) * scale).astype(np.float32)
    s = (np.sin(ph) * scale).astype(np.float32)
    right, left = [], []
    for sign in (1.0, -1.0):
        left.append(np.block([[c, sign * s], [-sign * s, c]]))
        big = np.zeros((256, 256), np.float32)
        for p in range(2):
            a = slice(p * G, p * G + G)
            b = slice(L + p * G, L + p * G + G)
            big[a, a] = c
            big[b, b] = c
            big[b, a] = sign * s
            big[a, b] = -sign * s
        right.append(big)
    return np.stack(left).astype(jnp.bfloat16), np.stack(right).astype(jnp.bfloat16)


def dot(a, b):
    return jnp.dot(a, b, preferred_element_type=jnp.float32)


def lanes():
    return lax.broadcasted_iota(jnp.int32, (G, L), 1)


def roll(v, s):
    s = s % L
    return v if s == 0 else pltpu.roll(v, s, 1)


def piece(tiles, j):
    o, t = (G * j) % L, (G * j) // L
    v = tiles[t]
    if o + G > L:
        v = jnp.where(lanes() >= o, v, tiles[t + 1])
    return v, o


def spread(tiles_a, tiles_b, j):
    a, o = piece(tiles_a, j)
    b, _ = piece(tiles_b, j)
    return jnp.where(lanes() < G, roll(a, -o), roll(b, G - o))


def load_tiles(ref, g, dt):
    base = g * 384 if isinstance(g, int) else pl.multiple_of(g * 384, 128)
    v = ref[:, pl.ds(base, 384)].astype(dt)
    return [v[:, i * L:(i + 1) * L] for i in range(3)]


def rows(i):
    if isinstance(i, int):
        return pl.ds(i * G, G)
    return pl.ds(pl.multiple_of(i * G, 16), G)


def relayout_targets(loc, tgt, dt):
    def body(g, _):
        for c in range(2):
            ta = load_tiles(loc.at[0, c], g, dt)
            tb = load_tiles(loc.at[1, c], g, dt)
            for j in range(8):
                tgt[c, rows(g * 8 + j), :] = spread(ta, tb, j).astype(jnp.bfloat16)
        return 0
    lax.fori_loop(0, 6, body, 0)


def make_kern(kern, s, q):
    def f(n):
        return ((n + G // 2) % G - G // 2).astype(jnp.float32)
    ly = lax.broadcasted_iota(jnp.int32, (G, L), 0)
    lz = lanes() % G
    yz = (f(ly) + q[1]) ** 2 + (f(lz) + q[2]) ** 2
    def body(x, _):
        kx = (f(x) + q[0]) ** 2
        kern[s, rows(x), :] = -4.0 / (kx + yz + 0.5)
        return 0
    lax.fori_loop(0, G, body, 0)


def pair_rhs(re0, re1, im0, im1):
    return jnp.concatenate(
        [jnp.concatenate([re0, re1], 1), jnp.concatenate([im0, im1], 1)], 0)


def phase_a(src, tgt, spr, b, left, right):
    bf = jnp.bfloat16
    rhs = []
    for g in range(6):
        tl = [load_tiles(src.at[c], g, bf) for c in range(2)]
        d = []
        for i in range(8):
            r = rows(g * 8 + i)
            m = [spread(tl[c], tl[c], i) for c in range(2)]
            spr[0, r, :] = m[0]
            spr[1, r, :] = m[1]
            mr, mi = m[0].astype(jnp.float32), m[1].astype(jnp.float32)
            tr, ti = tgt[0, r, :].astype(jnp.float32), tgt[1, r, :].astype(jnp.float32)
            d.append(jnp.concatenate([(mr * tr + mi * ti).astype(bf), (mr * ti - mi * tr).astype(bf)], 1))
        rhs.append(jnp.concatenate(d, 0))
    z = dot(jnp.concatenate(rhs, 0), right[0]).astype(bf)
    for y in range(0, G, 2):
        w = z[y * G:(y + 2) * G]
        o = dot(left[0], pair_rhs(w[:G, :L], w[G:, :L], w[:G, L:], w[G:, L:]))
        for i in range(2):
            for c in range(2):
                b[c, pl.ds(y + i, G, stride=G), :] = o[c * G:(c + 1) * G, i * L:(i + 1) * L]


def phase_b(b, cc, kern, left):
    bf = jnp.bfloat16
    for x in range(0, G, 2):
        v = [[b[c, rows(x + i), :].astype(bf) for i in range(2)] for c in range(2)]
        o = dot(left[0], pair_rhs(v[0][0], v[0][1], v[1][0], v[1][1]))
        k = jnp.concatenate([kern[rows(x), :], kern[rows(x + 1), :]], 1)
        o = dot(left[1], (o * jnp.concatenate([k, k], 0)).astype(bf))
        for i in range(2):
            for c in range(2):
                cc[c, pl.ds(x + i, G, stride=G), :] = o[c * G:(c + 1) * G, i * L:(i + 1) * L]


def phase_c(cc, spr, acc, left, right):
    bf = jnp.bfloat16
    n = 16
    def along_x(k):
        lhs = []
        for y in range(k * n, k * n + n, 2):
            v = [[cc[c, rows(y + i), :].astype(bf) for i in range(2)] for c in range(2)]
            o = dot(left[1], pair_rhs(v[0][0], v[0][1], v[1][0], v[1][1])).astype(bf)
            lhs += [jnp.concatenate([o[:G, :L], o[G:, :L]], 1), jnp.concatenate([o[:G, L:], o[G:, L:]], 1)]
        return jnp.concatenate(lhs, 0)
    lhs = along_x(0)
    for k in range(G // n):
        later = along_x(k + 1) if k + 1 < G // n else None
        p = dot(lhs, right[1])
        r = pl.ds(k * n * G, n * G)
        vr, vi = p[:, :L], p[:, L:]
        mr, mi = spr[0, r, :].astype(jnp.float32), spr[1, r, :].astype(jnp.float32)
        acc[0, r, :] += mr * vr - mi * vi
        acc[1, r, :] += mr * vi + mi * vr
        lhs = later


def gather_out(acc, out, dt):
    def body(g, _):
        ln = lanes()
        for c in range(2):
            a = [acc[c, rows(g * 8 + j), :].astype(dt) for j in range(8)]
            for p in range(2):
                tiles = [None] * 3
                for j in range(8):
                    o, t = (G * j) % L, (G * j) // L
                    r = roll(a[j], o - G * p)
                    tiles[t] = r if tiles[t] is None else jnp.where(ln >= o, r, tiles[t])
                    if o + G > L:
                        tiles[t + 1] = r
                base = pl.multiple_of(g * 384, 128)
                for t in range(3):
                    out[p, c, :, pl.ds(base + t * L, L)] = tiles[t].astype(jnp.bfloat16)
        return 0
    lax.fori_loop(0, 6, body, 0)


def kernel(loc, koff, umk, left_in, right_in, out, src, tgt, spr, b, cc, acc, kern, mine, left, right, held, ks, us,
           local, first, seeded, seed_send, pieces, across, twin, sends):
    band, kpt = lax.axis_index("band"), lax.axis_index("kpt")
    nk = lax.axis_size("kpt")
    x, zl, core = band // 16, (band // 2) % 8, band % 2
    after, before = lax.rem(kpt + 1, nk), lax.rem(kpt + nk - 1, nk)
    is_root = band == ROOT

    def at(bx, bz, bc):
        return bx * 16 + bz * 2 + bc

    def xat(d):
        return lax.rem(x + d, 4)

    def site(s, u, q, r):
        return src.at[s, u, q // 2, pl.ds(r * 16, 16), pl.ds(pl.multiple_of((q % 2) * HALF, 128), HALF)]

    def held_piece(q, r):
        return held.at[q // 2, pl.ds(r * 16, 16), pl.ds((q % 2) * HALF, HALF)]

    def remote(source, target, send, recv, b_, k_=kpt):
        return pltpu.make_async_remote_copy(
            src_ref=source, dst_ref=target, send_sem=send, recv_sem=recv,
            device_id={"band": b_, "kpt": k_}, device_id_type=MESH)

    def from_root(s, u, q, r):
        own = s == 0 and u == 0
        target = site(s, u, q, r) if own else held_piece(q, r)
        to = at(q, place(s, r, kpt), 0) if own else at(SEEDS[s][u][0], seed_z(s, after), u)
        return remote(
            loc.at[u, q // 2, pl.ds(r * 16, 16), pl.ds((q % 2) * HALF, HALF)], target,
            first.at[s * 2 + u, q, r], pieces.at[s, r] if own else seeded.at[q, r], to, kpt if s == 0 else after)

    def from_seed(s, u, q, r):
        return remote(held_piece(q, r), site(s, u, q, r), seed_send.at[q, r], pieces.at[s, r], at(q, place(s, r, kpt), u))

    def column(s, r, d):
        ref = site(s, core, x, r)
        return remote(ref, ref, sends.at[s, d - 1], pieces.at[s, r], at(x, lax.rem(zl + d, 8), core))

    def row(s, r, d):
        ref = site(s, core, x, r)
        return remote(ref, ref, sends.at[s, 7 + r * 3 + d - 1], across.at[s, r, d - 1], at(xat(d), zl, core))

    def arrived(s, r, d):
        ref = site(s, core, xat(4 - d), r)
        return remote(ref, ref, sends.at[s, 7 + r * 3 + d - 1], across.at[s, r, d - 1], at(xat(d), zl, core))

    def to_twin(s, r, d, u):
        ref = site(s, u, xat(4 - d) if d else x, r)
        return remote(ref, ref, sends.at[s, 16 + r * 4 + d], twin.at[s, r, d], at(x, zl, 1 - core))

    def seed_z(s, k):
        return jnp.where(lax.rem(k, 4) == 0, 7, 0) if s else 0

    def place(s, r, k):
        return jnp.where(seed_z(s, k) == 7, 7 - RELAYS[r], RELAYS[r])

    relay = [[zl == place(s, r, kpt) for r in range(3)] for s in range(2)]
    any_relay = [relay[s][0] | relay[s][1] | relay[s][2] for s in range(2)]
    seeds = [(s, u, (x == SEEDS[s][u][0]) & (zl == seed_z(s, kpt)) & (core == u)) for s, u in ((0, 1), (1, 0), (1, 1))]
    any_seed = seeds[0][2] | seeds[1][2] | seeds[2][2]

    bar = pltpu.get_barrier_semaphore()

    def greet(b_, k_=kpt):
        pl.semaphore_signal(bar, inc=1, device_id={"band": b_, "kpt": k_}, device_id_type=MESH)

    for s in range(2):
        @pl.when(any_relay[s])
        def _():
            greet(jnp.where(core == 0, at(SEEDS[s][0][0], seed_z(s, kpt), 0), at(SEEDS[s][1][0], seed_z(s, kpt), 1)))

    for s, u, here in seeds:
        @pl.when(here)
        def _():
            greet(ROOT, kpt if s == 0 else before)

    for s in range(2):
        for r in range(3):
            @pl.when(jnp.logical_not(relay[s][r]))
            def _():
                greet(at(x, place(s, r, kpt), core))
    for d in range(1, 4):
        greet(at(xat(d), zl, core))
    greet(at(x, zl, 1 - core))

    copies = [pltpu.make_async_copy(a, c, local.at[i]) for i, (a, c) in enumerate(
        ((loc, mine), (left_in, left), (right_in, right), (koff, ks), (umk, us)))]
    for c in copies:
        c.start()

    @pl.when(any_relay[0] ^ any_relay[1])
    def _():
        pl.semaphore_wait(bar, 11)

    @pl.when(any_relay[0] & any_relay[1])
    def _():
        pl.semaphore_wait(bar, 18)

    @pl.when(any_seed)
    def _():
        pl.semaphore_wait(bar, 16)

    @pl.when(is_root)
    def _():
        pl.semaphore_wait(bar, 19)

    @pl.when(jnp.logical_not(any_relay[0] | any_relay[1] | any_seed | is_root))
    def _():
        pl.semaphore_wait(bar, 4)

    def each_piece(f):
        for r in range(3):
            for q in range(4):
                f(q, r)

    @pl.when(is_root)
    def _():
        each_piece(lambda q, r: [from_root(s, u, q, r).start() for s, u in ((0, 0), (0, 1))])
        each_piece(lambda q, r: [from_root(s, u, q, r).start() for s, u in ((1, 0), (1, 1))])

    for c in copies:
        c.wait()
    relayout_targets(mine, tgt, jnp.bfloat16)
    for s in range(2):
        other = lax.rem(kpt + nk - s, nk)
        make_kern(kern, s, [0.5 * (ks[i, kpt] - ks[i, other]).astype(jnp.float32) + us[s, i].astype(jnp.float32) for i in range(3)])
    acc[...] = jnp.zeros_like(acc)

    for s, u, here in seeds:
        @pl.when(here)
        def _():
            def pass_on(q, r):
                from_root(s, u, q, r).wait_recv()
                from_seed(s, u, q, r).start()
            each_piece(pass_on)

    def spread_piece(s, r):
        for d in (2, 1, 3):
            row(s, r, d).start()
        to_twin(s, r, 0, core).start()

    def lead(s):
        for r in range(3):
            @pl.when(relay[s][r])
            def _():
                column(s, r, 1).wait_recv()
                for d in range(1, 8):
                    column(s, r, d).start()
                spread_piece(s, r)

    def rest(s):
        for r in range(3):
            @pl.when(jnp.logical_not(relay[s][r]))
            def _():
                column(s, r, 1).wait_recv()
                spread_piece(s, r)

    def take(s):
        for r in range(3):
            for d in (1, 3, 2):
                arrived(s, r, d).wait_recv()
                to_twin(s, r, d, core).start()

    def finish(s):
        for r in range(3):
            for d in range(4):
                to_twin(s, r, d, 1 - core).wait_recv()

    lead(0)
    rest(0)
    lead(1)
    take(0)

    def one(u, _):
        m = lax.rem(core + u, 2)

        @pl.when(u == 1)
        def _():
            finish(0)

        @pl.when(u == 3)
        def _():
            finish(1)

        phase_a(src.at[u // 2, m], tgt, spr, b, left, right)

        @pl.when(u == 0)
        def _():
            rest(1)

        phase_b(b, cc, kern.at[u // 2], left)

        @pl.when(u == 1)
        def _():
            take(1)

        phase_c(cc, spr, acc, left, right)
        return 0

    lax.fori_loop(0, 4, one, 0)
    gather_out(acc, out, jnp.float32)

    @pl.when(is_root)
    def _():
        each_piece(lambda q, r: [from_root(s, u, q, r).wait_send() for s in range(2) for u in range(2)])

    @pl.when(any_seed)
    def _():
        each_piece(lambda q, r: from_seed(0, 1, q, r).wait_send())

    for s in range(2):
        @pl.when(any_relay[s])
        def _():
            for d in range(1, 8):
                column(s, 0, d).wait_send()
        for r in range(3):
            for d in range(1, 4):
                row(s, r, d).wait_send()
            for d in range(4):
                to_twin(s, r, d, core).wait_send()


def on_device(orbitals, koff, umklapp):
    bf = jnp.bfloat16
    loc = orbitals[0]
    left, right = tables()
    hbm = pl.BlockSpec(memory_space=pl.ANY)
    dma = pltpu.SemaphoreType.DMA
    cube = (2, G * G, L)
    res = pl.pallas_call(
        kernel,
        out_shape=jax.ShapeDtypeStruct(loc.shape, bf),
        in_specs=[hbm] * 5,
        out_specs=pl.BlockSpec(memory_space=pltpu.VMEM),
        scratch_shapes=[pltpu.VMEM((2,) + loc.shape, bf), pltpu.VMEM(cube, bf), pltpu.VMEM(cube, bf)]
        + [pltpu.VMEM(cube, jnp.float32)] * 4
        + [pltpu.VMEM(loc.shape, bf), pltpu.VMEM(left.shape, bf), pltpu.VMEM(right.shape, bf), pltpu.VMEM(loc.shape[1:], bf)]
        + [pltpu.SMEM((3, koff.shape[0]), jnp.int32), pltpu.SMEM(umklapp.shape[1:], jnp.int32)]
        + [dma((5,)), dma((4, 4, 3)), dma((4, 3)), dma((4, 3)), dma((2, 3)), dma((2, 3, 3)), dma((2, 3, 4)), dma((2, 28))],
        compiler_params=pltpu.CompilerParams(collective_id=0, has_side_effects=True, vmem_limit_bytes=56 * 2**20),
    )(loc, koff.T, umklapp[0], jnp.asarray(left), jnp.asarray(right))
    return res[None]


def solution(mesh):
    return jax.shard_map(
        on_device,
        mesh=mesh,
        in_specs=(P("kpt", "band", None, None, None), P(), P("kpt", None, None)),
        out_specs=P("kpt", "band", None, None, None),
        check_vma=False,
    )
```

```python
import math

import jax
import jax.numpy as jnp
import numpy as np
from jax import lax
from jax.experimental import pallas as pl
from jax.experimental.pallas import tpu as pltpu
from jax.sharding import PartitionSpec as P

MESH = pl.DeviceIdType.MESH
KSTEPS = 2
RELAYS = (5, 3, 1)
HALF = 1152
ROOT = 32
SEEDS = ((2, 0), (3, 1)), ((1, 0), (0, 1))

G = 48
L = 128


def tables():
    idx = np.arange(G)
    ph = (idx[:, None] * idx[None, :] % G).astype(np.float32) * np.float32(2.0 * math.pi / G)
    scale = np.float32(1.0 / math.sqrt(G))
    c = (np.cos(ph) * scale).astype(np.float32)
    s = (np.sin(ph) * scale).astype(np.float32)
    right, left = [], []
    for sign in (1.0, -1.0):
        left.append(np.block([[c, sign * s], [-sign * s, c]]))
        big = np.zeros((256, 256), np.float32)
        for p in range(2):
            a = slice(p * G, p * G + G)
            b = slice(L + p * G, L + p * G + G)
            big[a, a] = c
            big[b, b] = c
            big[b, a] = sign * s
            big[a, b] = -sign * s
        right.append(big)
    return np.stack(left).astype(jnp.bfloat16), np.stack(right).astype(jnp.bfloat16)


def dot(a, b):
    return jnp.dot(a, b, preferred_element_type=jnp.float32)


def lanes():
    return lax.broadcasted_iota(jnp.int32, (G, L), 1)


def roll(v, s):
    s = s % L
    return v if s == 0 else pltpu.roll(v, s, 1)


def piece(tiles, j):
    o, t = (G * j) % L, (G * j) // L
    v = tiles[t]
    if o + G > L:
        v = jnp.where(lanes() >= o, v, tiles[t + 1])
    return v, o


def spread(tiles_a, tiles_b, j):
    a, o = piece(tiles_a, j)
    b, _ = piece(tiles_b, j)
    return jnp.where(lanes() < G, roll(a, -o), roll(b, G - o))


def load_tiles(ref, g, dt):
    base = g * 384 if isinstance(g, int) else pl.multiple_of(g * 384, 128)
    v = ref[:, pl.ds(base, 384)].astype(dt)
    return [v[:, i * L:(i + 1) * L] for i in range(3)]


def rows(i):
    if isinstance(i, int):
        return pl.ds(i * G, G)
    return pl.ds(pl.multiple_of(i * G, 16), G)


def relayout_targets(loc, tgt, dt):
    def body(g, _):
        for c in range(2):
            ta = load_tiles(loc.at[0, c], g, dt)
            tb = load_tiles(loc.at[1, c], g, dt)
            for j in range(8):
                tgt[c, rows(g * 8 + j), :] = spread(ta, tb, j).astype(jnp.bfloat16)
        return 0
    lax.fori_loop(0, 6, body, 0)


def make_kern(kern, s, q):
    def f(n):
        return ((n + G // 2) % G - G // 2).astype(jnp.float32)
    ly = lax.broadcasted_iota(jnp.int32, (G, L), 0)
    lz = lanes() % G
    yz = (f(ly) + q[1]) ** 2 + (f(lz) + q[2]) ** 2
    def body(x, _):
        kx = (f(x) + q[0]) ** 2
        kern[s, rows(x), :] = -4.0 / (kx + yz + 0.5)
        return 0
    lax.fori_loop(0, G, body, 0)


def pair_rhs(re0, re1, im0, im1):
    return jnp.concatenate(
        [jnp.concatenate([re0, re1], 1), jnp.concatenate([im0, im1], 1)], 0)


def phase_a(src, tgt, spr, b, left, right):
    bf = jnp.bfloat16
    rhs = []
    for g in range(6):
        tl = [load_tiles(src.at[c], g, bf) for c in range(2)]
        d = []
        for i in range(8):
            r = rows(g * 8 + i)
            m = [spread(tl[c], tl[c], i) for c in range(2)]
            spr[0, r, :] = m[0]
            spr[1, r, :] = m[1]
            mr, mi = m[0].astype(jnp.float32), m[1].astype(jnp.float32)
            tr, ti = tgt[0, r, :].astype(jnp.float32), tgt[1, r, :].astype(jnp.float32)
            d.append(jnp.concatenate([(mr * tr + mi * ti).astype(bf), (mr * ti - mi * tr).astype(bf)], 1))
        rhs.append(jnp.concatenate(d, 0))
    z = dot(jnp.concatenate(rhs, 0), right[0]).astype(bf)
    for y in range(0, G, 2):
        w = z[y * G:(y + 2) * G]
        o = dot(left[0], pair_rhs(w[:G, :L], w[G:, :L], w[:G, L:], w[G:, L:]))
        for i in range(2):
            for c in range(2):
                b[c, pl.ds(y + i, G, stride=G), :] = o[c * G:(c + 1) * G, i * L:(i + 1) * L]


def phase_b(b, cc, kern, left):
    bf = jnp.bfloat16
    for x in range(0, G, 2):
        v = [[b[c, rows(x + i), :].astype(bf) for i in range(2)] for c in range(2)]
        o = dot(left[0], pair_rhs(v[0][0], v[0][1], v[1][0], v[1][1]))
        k = jnp.concatenate([kern[rows(x), :], kern[rows(x + 1), :]], 1)
        o = dot(left[1], (o * jnp.concatenate([k, k], 0)).astype(bf))
        for i in range(2):
            for c in range(2):
                cc[c, pl.ds(x + i, G, stride=G), :] = o[c * G:(c + 1) * G, i * L:(i + 1) * L]


def phase_c(cc, spr, acc, left, right):
    bf = jnp.bfloat16
    n = 16
    def along_x(k):
        lhs = []
        for y in range(k * n, k * n + n, 2):
            v = [[cc[c, rows(y + i), :].astype(bf) for i in range(2)] for c in range(2)]
            o = dot(left[1], pair_rhs(v[0][0], v[0][1], v[1][0], v[1][1])).astype(bf)
            lhs += [jnp.concatenate([o[:G, :L], o[G:, :L]], 1), jnp.concatenate([o[:G, L:], o[G:, L:]], 1)]
        return jnp.concatenate(lhs, 0)
    lhs = along_x(0)
    for k in range(G // n):
        later = along_x(k + 1) if k + 1 < G // n else None
        p = dot(lhs, right[1])
        r = pl.ds(k * n * G, n * G)
        vr, vi = p[:, :L], p[:, L:]
        mr, mi = spr[0, r, :].astype(jnp.float32), spr[1, r, :].astype(jnp.float32)
        acc[0, r, :] += mr * vr - mi * vi
        acc[1, r, :] += mr * vi + mi * vr
        lhs = later


def gather_out(acc, out, dt):
    def body(g, _):
        ln = lanes()
        for c in range(2):
            a = [acc[c, rows(g * 8 + j), :].astype(dt) for j in range(8)]
            for p in range(2):
                tiles = [None] * 3
                for j in range(8):
                    o, t = (G * j) % L, (G * j) // L
                    r = roll(a[j], o - G * p)
                    tiles[t] = r if tiles[t] is None else jnp.where(ln >= o, r, tiles[t])
                    if o + G > L:
                        tiles[t + 1] = r
                base = pl.multiple_of(g * 384, 128)
                for t in range(3):
                    out[p, c, :, pl.ds(base + t * L, L)] = tiles[t].astype(jnp.bfloat16)
        return 0
    lax.fori_loop(0, 6, body, 0)


def kernel(loc, koff, umk, left_in, right_in, out, src, tgt, spr, b, cc, acc, kern, mine, left, right, held, ks, us,
           local, first, seeded, seed_send, pieces, across, twin, sends):
    band, kpt = lax.axis_index("band"), lax.axis_index("kpt")
    nk = lax.axis_size("kpt")
    x, zl, core = band // 16, (band // 2) % 8, band % 2
    after, before = lax.rem(kpt + 1, nk), lax.rem(kpt + nk - 1, nk)
    is_root = band == ROOT

    def at(bx, bz, bc):
        return bx * 16 + bz * 2 + bc

    def xat(d):
        return lax.rem(x + d, 4)

    def site(s, u, q, r):
        return src.at[s, u, q // 2, pl.ds(r * 16, 16), pl.ds(pl.multiple_of((q % 2) * HALF, 128), HALF)]

    def held_piece(q, r):
        return held.at[q // 2, pl.ds(r * 16, 16), pl.ds((q % 2) * HALF, HALF)]

    def remote(source, target, send, recv, b_, k_=kpt):
        return pltpu.make_async_remote_copy(
            src_ref=source, dst_ref=target, send_sem=send, recv_sem=recv,
            device_id={"band": b_, "kpt": k_}, device_id_type=MESH)

    def from_root(s, u, q, r):
        own = s == 0 and u == 0
        target = site(s, u, q, r) if own else held_piece(q, r)
        to = at(q, place(s, r, kpt), 0) if own else at(SEEDS[s][u][0], seed_z(s, after), u)
        return remote(
            loc.at[u, q // 2, pl.ds(r * 16, 16), pl.ds((q % 2) * HALF, HALF)], target,
            first.at[s * 2 + u, q, r], pieces.at[s, r] if own else seeded.at[q, r], to, kpt if s == 0 else after)

    def onward(q, r):
        return remote(
            held_piece(q, r), held_piece(q, r), first.at[3, q, r], seeded.at[q, r],
            at(SEEDS[1][1][0], seed_z(1, after), 1), after)

    def from_seed(s, u, q, r):
        return remote(held_piece(q, r), site(s, u, q, r), seed_send.at[q, r], pieces.at[s, r], at(q, place(s, r, kpt), u))

    def column(s, r, d):
        ref = site(s, core, x, r)
        return remote(ref, ref, sends.at[s, d - 1], pieces.at[s, r], at(x, lax.rem(zl + d, 8), core))

    def row(s, r, d):
        ref = site(s, core, x, r)
        return remote(ref, ref, sends.at[s, 7 + r * 3 + d - 1], across.at[s, r, d - 1], at(xat(d), zl, core))

    def arrived(s, r, d):
        ref = site(s, core, xat(4 - d), r)
        return remote(ref, ref, sends.at[s, 7 + r * 3 + d - 1], across.at[s, r, d - 1], at(xat(d), zl, core))

    def to_twin(s, r, d, u):
        ref = site(s, u, xat(4 - d) if d else x, r)
        return remote(ref, ref, sends.at[s, 16 + r * 4 + d], twin.at[s, r, d], at(x, zl, 1 - core))

    def seed_z(s, k):
        return jnp.where(lax.rem(k, 4) == 0, 7, 0) if s else 0

    def place(s, r, k):
        return jnp.where(seed_z(s, k) == 7, 7 - RELAYS[r], RELAYS[r])

    relay = [[zl == place(s, r, kpt) for r in range(3)] for s in range(2)]
    any_relay = [relay[s][0] | relay[s][1] | relay[s][2] for s in range(2)]
    seeds = [(s, u, (x == SEEDS[s][u][0]) & (zl == seed_z(s, kpt)) & (core == u)) for s, u in ((0, 1), (1, 0), (1, 1))]
    any_seed = seeds[0][2] | seeds[1][2] | seeds[2][2]

    bar = pltpu.get_barrier_semaphore()

    def greet(b_, k_=kpt):
        pl.semaphore_signal(bar, inc=1, device_id={"band": b_, "kpt": k_}, device_id_type=MESH)

    for s in range(2):
        @pl.when(any_relay[s])
        def _():
            greet(jnp.where(core == 0, at(SEEDS[s][0][0], seed_z(s, kpt), 0), at(SEEDS[s][1][0], seed_z(s, kpt), 1)))

    for s, u, here in seeds:
        @pl.when(here)
        def _():
            greet(at(SEEDS[0][1][0], 0, 1) if s and u else ROOT, before if s else kpt)

    for s in range(2):
        for r in range(3):
            @pl.when(jnp.logical_not(relay[s][r]))
            def _():
                greet(at(x, place(s, r, kpt), core))
    for d in range(1, 4):
        greet(at(xat(d), zl, core))
    greet(at(x, zl, 1 - core))

    copies = [pltpu.make_async_copy(a, c, local.at[i]) for i, (a, c) in enumerate(
        ((loc, mine), (left_in, left), (right_in, right), (koff, ks), (umk, us)))]
    for c in copies:
        c.start()

    @pl.when(any_relay[0] ^ any_relay[1])
    def _():
        pl.semaphore_wait(bar, 11)

    @pl.when(any_relay[0] & any_relay[1])
    def _():
        pl.semaphore_wait(bar, 18)

    @pl.when(seeds[0][2])
    def _():
        pl.semaphore_wait(bar, 17)

    @pl.when(seeds[1][2] | seeds[2][2])
    def _():
        pl.semaphore_wait(bar, 16)

    @pl.when(is_root)
    def _():
        pl.semaphore_wait(bar, 18)

    @pl.when(jnp.logical_not(any_relay[0] | any_relay[1] | any_seed | is_root))
    def _():
        pl.semaphore_wait(bar, 4)

    def each_piece(f):
        for r in range(3):
            for q in range(4):
                f(q, r)

    @pl.when(is_root)
    def _():
        each_piece(lambda q, r: [from_root(s, u, q, r).start() for s, u in ((0, 1), (0, 0), (1, 0))])

    for c in copies:
        c.wait()
    relayout_targets(mine, tgt, jnp.bfloat16)
    for s in range(2):
        other = lax.rem(kpt + nk - s, nk)
        make_kern(kern, s, [0.5 * (ks[i, kpt] - ks[i, other]).astype(jnp.float32) + us[s, i].astype(jnp.float32) for i in range(3)])
    acc[...] = jnp.zeros_like(acc)

    for s, u, here in seeds:
        @pl.when(here)
        def _():
            def pass_on(q, r):
                from_root(s, u, q, r).wait_recv()
                from_seed(s, u, q, r).start()
                if s == 0:
                    onward(q, r).start()
            each_piece(pass_on)

    def spread_piece(s, r):
        for d in (2, 1, 3):
            row(s, r, d).start()
        to_twin(s, r, 0, core).start()

    def lead(s):
        for r in range(3):
            @pl.when(relay[s][r])
            def _():
                column(s, r, 1).wait_recv()
                for d in range(1, 8):
                    column(s, r, d).start()
                spread_piece(s, r)

    def rest(s):
        for r in range(3):
            @pl.when(jnp.logical_not(relay[s][r]))
            def _():
                column(s, r, 1).wait_recv()
                spread_piece(s, r)

    def take(s):
        for r in range(3):
            for d in (1, 3, 2):
                arrived(s, r, d).wait_recv()
                to_twin(s, r, d, core).start()

    def finish(s):
        for r in range(3):
            for d in range(4):
                to_twin(s, r, d, 1 - core).wait_recv()

    lead(0)
    rest(0)
    lead(1)
    take(0)

    def one(u, _):
        m = lax.rem(core + u, 2)

        @pl.when(u == 1)
        def _():
            finish(0)

        @pl.when(u == 3)
        def _():
            finish(1)

        phase_a(src.at[u // 2, m], tgt, spr, b, left, right)

        @pl.when(u == 0)
        def _():
            rest(1)

        phase_b(b, cc, kern.at[u // 2], left)

        @pl.when(u == 1)
        def _():
            take(1)

        phase_c(cc, spr, acc, left, right)
        return 0

    lax.fori_loop(0, 4, one, 0)
    gather_out(acc, out, jnp.float32)

    @pl.when(is_root)
    def _():
        each_piece(lambda q, r: [from_root(s, u, q, r).wait_send() for s, u in ((0, 1), (0, 0), (1, 0))])

    @pl.when(any_seed)
    def _():
        each_piece(lambda q, r: from_seed(0, 1, q, r).wait_send())

    @pl.when(seeds[0][2])
    def _():
        each_piece(lambda q, r: onward(q, r).wait_send())

    for s in range(2):
        @pl.when(any_relay[s])
        def _():
            for d in range(1, 8):
                column(s, 0, d).wait_send()
        for r in range(3):
            for d in range(1, 4):
                row(s, r, d).wait_send()
            for d in range(4):
                to_twin(s, r, d, core).wait_send()


def on_device(orbitals, koff, umklapp):
    bf = jnp.bfloat16
    loc = orbitals[0]
    left, right = tables()
    hbm = pl.BlockSpec(memory_space=pl.ANY)
    dma = pltpu.SemaphoreType.DMA
    cube = (2, G * G, L)
    res = pl.pallas_call(
        kernel,
        out_shape=jax.ShapeDtypeStruct(loc.shape, bf),
        in_specs=[hbm] * 5,
        out_specs=pl.BlockSpec(memory_space=pltpu.VMEM),
        scratch_shapes=[pltpu.VMEM((2,) + loc.shape, bf), pltpu.VMEM(cube, bf), pltpu.VMEM(cube, bf)]
        + [pltpu.VMEM(cube, jnp.float32)] * 4
        + [pltpu.VMEM(loc.shape, bf), pltpu.VMEM(left.shape, bf), pltpu.VMEM(right.shape, bf), pltpu.VMEM(loc.shape[1:], bf)]
        + [pltpu.SMEM((3, koff.shape[0]), jnp.int32), pltpu.SMEM(umklapp.shape[1:], jnp.int32)]
        + [dma((5,)), dma((4, 4, 3)), dma((4, 3)), dma((4, 3)), dma((2, 3)), dma((2, 3, 3)), dma((2, 3, 4)), dma((2, 28))],
        compiler_params=pltpu.CompilerParams(collective_id=0, has_side_effects=True, vmem_limit_bytes=56 * 2**20),
    )(loc, koff.T, umklapp[0], jnp.asarray(left), jnp.asarray(right))
    return res[None]


def solution(mesh):
    return jax.shard_map(
        on_device,
        mesh=mesh,
        in_specs=(P("kpt", "band", None, None, None), P(), P("kpt", None, None)),
        out_specs=P("kpt", "band", None, None, None),
        check_vma=False,
    )
```

```python
import math

import jax
import jax.numpy as jnp
import numpy as np
from jax import lax
from jax.experimental import pallas as pl
from jax.experimental.pallas import tpu as pltpu
from jax.sharding import PartitionSpec as P

MESH = pl.DeviceIdType.MESH
KSTEPS = 2
RELAYS = (5, 3, 1)
HALF = 1152
ROOT = 32
SEEDS = ((2, 0), (3, 1)), ((1, 0), (0, 1))

G = 48
L = 128


def tables():
    idx = np.arange(G)
    ph = (idx[:, None] * idx[None, :] % G).astype(np.float32) * np.float32(2.0 * math.pi / G)
    scale = np.float32(1.0 / math.sqrt(G))
    c = (np.cos(ph) * scale).astype(np.float32)
    s = (np.sin(ph) * scale).astype(np.float32)
    right, left = [], []
    for sign in (1.0, -1.0):
        left.append(np.block([[c, sign * s], [-sign * s, c]]))
        big = np.zeros((256, 256), np.float32)
        for p in range(2):
            a = slice(p * G, p * G + G)
            b = slice(L + p * G, L + p * G + G)
            big[a, a] = c
            big[b, b] = c
            big[b, a] = sign * s
            big[a, b] = -sign * s
        right.append(big)
    return np.stack(left).astype(jnp.bfloat16), np.stack(right).astype(jnp.bfloat16)


def dot(a, b):
    return jnp.dot(a, b, preferred_element_type=jnp.float32)


def lanes():
    return lax.broadcasted_iota(jnp.int32, (G, L), 1)


def roll(v, s):
    s = s % L
    return v if s == 0 else pltpu.roll(v, s, 1)


def piece(tiles, j):
    o, t = (G * j) % L, (G * j) // L
    v = tiles[t]
    if o + G > L:
        v = jnp.where(lanes() >= o, v, tiles[t + 1])
    return v, o


def spread(tiles_a, tiles_b, j):
    a, o = piece(tiles_a, j)
    b, _ = piece(tiles_b, j)
    return jnp.where(lanes() < G, roll(a, -o), roll(b, G - o))


def load_tiles(ref, g, dt):
    base = g * 384 if isinstance(g, int) else pl.multiple_of(g * 384, 128)
    v = ref[:, pl.ds(base, 384)].astype(dt)
    return [v[:, i * L:(i + 1) * L] for i in range(3)]


def rows(i):
    if isinstance(i, int):
        return pl.ds(i * G, G)
    return pl.ds(pl.multiple_of(i * G, 16), G)


def relayout_targets(loc, tgt, dt):
    def body(g, _):
        for c in range(2):
            ta = load_tiles(loc.at[0, c], g, dt)
            tb = load_tiles(loc.at[1, c], g, dt)
            for j in range(8):
                tgt[c, rows(g * 8 + j), :] = spread(ta, tb, j).astype(jnp.bfloat16)
        return 0
    lax.fori_loop(0, 6, body, 0)


def make_kern(kern, s, q):
    def f(n):
        return ((n + G // 2) % G - G // 2).astype(jnp.float32)
    ly = lax.broadcasted_iota(jnp.int32, (G, L), 0)
    lz = lanes() % G
    yz = (f(ly) + q[1]) ** 2 + (f(lz) + q[2]) ** 2
    def body(x, _):
        kx = (f(x) + q[0]) ** 2
        kern[s, rows(x), :] = -4.0 / (kx + yz + 0.5)
        return 0
    lax.fori_loop(0, G, body, 0)


def pair_rhs(re0, re1, im0, im1):
    return jnp.concatenate(
        [jnp.concatenate([re0, re1], 1), jnp.concatenate([im0, im1], 1)], 0)


def phase_a(src, tgt, spr, b, left, right):
    bf = jnp.bfloat16
    rhs = []
    for g in range(6):
        tl = [load_tiles(src.at[c], g, bf) for c in range(2)]
        d = []
        for i in range(8):
            r = rows(g * 8 + i)
            m = [spread(tl[c], tl[c], i) for c in range(2)]
            spr[0, r, :] = m[0]
            spr[1, r, :] = m[1]
            mr, mi = m[0].astype(jnp.float32), m[1].astype(jnp.float32)
            tr, ti = tgt[0, r, :].astype(jnp.float32), tgt[1, r, :].astype(jnp.float32)
            d.append(jnp.concatenate([(mr * tr + mi * ti).astype(bf), (mr * ti - mi * tr).astype(bf)], 1))
        rhs.append(jnp.concatenate(d, 0))
    z = dot(jnp.concatenate(rhs, 0), right[0]).astype(bf)
    for y in range(0, G, 2):
        w = z[y * G:(y + 2) * G]
        o = dot(left[0], pair_rhs(w[:G, :L], w[G:, :L], w[:G, L:], w[G:, L:]))
        for i in range(2):
            for c in range(2):
                b[c, pl.ds(y + i, G, stride=G), :] = o[c * G:(c + 1) * G, i * L:(i + 1) * L]


def phase_b(b, cc, kern, left):
    bf = jnp.bfloat16
    for x in range(0, G, 2):
        v = [[b[c, rows(x + i), :].astype(bf) for i in range(2)] for c in range(2)]
        o = dot(left[0], pair_rhs(v[0][0], v[0][1], v[1][0], v[1][1]))
        k = jnp.concatenate([kern[rows(x), :], kern[rows(x + 1), :]], 1)
        o = dot(left[1], (o * jnp.concatenate([k, k], 0)).astype(bf))
        for i in range(2):
            for c in range(2):
                cc[c, pl.ds(x + i, G, stride=G), :] = o[c * G:(c + 1) * G, i * L:(i + 1) * L]


def phase_c(cc, spr, acc, left, right):
    bf = jnp.bfloat16
    n = 16
    def along_x(k):
        lhs = []
        for y in range(k * n, k * n + n, 2):
            v = [[cc[c, rows(y + i), :].astype(bf) for i in range(2)] for c in range(2)]
            o = dot(left[1], pair_rhs(v[0][0], v[0][1], v[1][0], v[1][1])).astype(bf)
            lhs += [jnp.concatenate([o[:G, :L], o[G:, :L]], 1), jnp.concatenate([o[:G, L:], o[G:, L:]], 1)]
        return jnp.concatenate(lhs, 0)
    lhs = along_x(0)
    for k in range(G // n):
        later = along_x(k + 1) if k + 1 < G // n else None
        p = dot(lhs, right[1])
        r = pl.ds(k * n * G, n * G)
        vr, vi = p[:, :L], p[:, L:]
        mr, mi = spr[0, r, :].astype(jnp.float32), spr[1, r, :].astype(jnp.float32)
        acc[0, r, :] += mr * vr - mi * vi
        acc[1, r, :] += mr * vi + mi * vr
        lhs = later


def gather_out(acc, out, dt):
    def body(g, _):
        ln = lanes()
        for c in range(2):
            a = [acc[c, rows(g * 8 + j), :].astype(dt) for j in range(8)]
            for p in range(2):
                tiles = [None] * 3
                for j in range(8):
                    o, t = (G * j) % L, (G * j) // L
                    r = roll(a[j], o - G * p)
                    tiles[t] = r if tiles[t] is None else jnp.where(ln >= o, r, tiles[t])
                    if o + G > L:
                        tiles[t + 1] = r
                base = pl.multiple_of(g * 384, 128)
                for t in range(3):
                    out[p, c, :, pl.ds(base + t * L, L)] = tiles[t].astype(jnp.bfloat16)
        return 0
    lax.fori_loop(0, 6, body, 0)


def kernel(loc, koff, umk, left_in, right_in, out, src, tgt, spr, b, cc, acc, kern, mine, left, right, held, ks, us,
           local, first, seeded, seed_send, pieces, across, twin, sends):
    band, kpt = lax.axis_index("band"), lax.axis_index("kpt")
    nk = lax.axis_size("kpt")
    x, zl, core = band // 16, (band // 2) % 8, band % 2
    after, before = lax.rem(kpt + 1, nk), lax.rem(kpt + nk - 1, nk)
    is_root = band == ROOT

    def at(bx, bz, bc):
        return bx * 16 + bz * 2 + bc

    def xat(d):
        return lax.rem(x + d, 4)

    def site(s, u, q, r):
        return src.at[s, u, q // 2, pl.ds(r * 16, 16), pl.ds(pl.multiple_of((q % 2) * HALF, 128), HALF)]

    def held_piece(q, r):
        return held.at[q // 2, pl.ds(r * 16, 16), pl.ds((q % 2) * HALF, HALF)]

    def remote(source, target, send, recv, b_, k_=kpt):
        return pltpu.make_async_remote_copy(
            src_ref=source, dst_ref=target, send_sem=send, recv_sem=recv,
            device_id={"band": b_, "kpt": k_}, device_id_type=MESH)

    def from_root(s, u, q, r):
        own = s == 0 and u == 0
        target = site(s, u, q, r) if own else held_piece(q, r)
        to = at(q, place(s, r, kpt), 0) if own else at(SEEDS[s][u][0], seed_z(s, after), u)
        return remote(
            loc.at[u, q // 2, pl.ds(r * 16, 16), pl.ds((q % 2) * HALF, HALF)], target,
            first.at[s * 2 + u, q, r], pieces.at[s, r] if own else seeded.at[q, r], to, kpt if s == 0 else after)

    def onward(q, r):
        return remote(
            held_piece(q, r), held_piece(q, r), first.at[3, q, r], seeded.at[q, r],
            at(SEEDS[1][1][0], seed_z(1, after), 1), after)

    def from_seed(s, u, q, r):
        return remote(held_piece(q, r), site(s, u, q, r), seed_send.at[q, r], pieces.at[s, r], at(q, place(s, r, kpt), u))

    def column(s, r, d):
        ref = site(s, core, x, r)
        return remote(ref, ref, sends.at[s, d - 1], pieces.at[s, r], at(x, lax.rem(zl + d, 8), core))

    def row(s, r, d):
        ref = site(s, core, x, r)
        return remote(ref, ref, sends.at[s, 7 + r * 3 + d - 1], across.at[s, r, d - 1], at(xat(d), zl, core))

    def arrived(s, r, d):
        ref = site(s, core, xat(4 - d), r)
        return remote(ref, ref, sends.at[s, 7 + r * 3 + d - 1], across.at[s, r, d - 1], at(xat(d), zl, core))

    def to_twin(s, r, d, u):
        ref = site(s, u, xat(4 - d) if d else x, r)
        return remote(ref, ref, sends.at[s, 16 + r * 4 + d], twin.at[s, r, d], at(x, zl, 1 - core))

    def seed_z(s, k):
        return jnp.where(lax.rem(k, 4) == 0, 7, 0) if s else 0

    def place(s, r, k):
        return jnp.where(seed_z(s, k) == 7, 7 - RELAYS[r], RELAYS[r])

    relay = [[zl == place(s, r, kpt) for r in range(3)] for s in range(2)]
    any_relay = [relay[s][0] | relay[s][1] | relay[s][2] for s in range(2)]
    seeds = [(s, u, (x == SEEDS[s][u][0]) & (zl == seed_z(s, kpt)) & (core == u)) for s, u in ((0, 1), (1, 0), (1, 1))]
    any_seed = seeds[0][2] | seeds[1][2] | seeds[2][2]

    bar = pltpu.get_barrier_semaphore()

    def greet(b_, k_=kpt):
        pl.semaphore_signal(bar, inc=1, device_id={"band": b_, "kpt": k_}, device_id_type=MESH)

    for s in range(2):
        @pl.when(any_relay[s])
        def _():
            greet(jnp.where(core == 0, at(SEEDS[s][0][0], seed_z(s, kpt), 0), at(SEEDS[s][1][0], seed_z(s, kpt), 1)))

    for s, u, here in seeds:
        @pl.when(here)
        def _():
            greet(at(SEEDS[0][1][0], 0, 1) if s and u else ROOT, before if s else kpt)

    for s in range(2):
        for r in range(3):
            @pl.when(jnp.logical_not(relay[s][r]))
            def _():
                greet(at(x, place(s, r, kpt), core))
    for d in range(1, 4):
        greet(at(xat(d), zl, core))
    greet(at(x, zl, 1 - core))

    copies = [pltpu.make_async_copy(a, c, local.at[i]) for i, (a, c) in enumerate(
        ((loc, mine), (left_in, left), (right_in, right), (koff, ks), (umk, us)))]
    for c in copies:
        c.start()

    @pl.when(any_relay[0] ^ any_relay[1])
    def _():
        pl.semaphore_wait(bar, 11)

    @pl.when(any_relay[0] & any_relay[1])
    def _():
        pl.semaphore_wait(bar, 18)

    @pl.when(seeds[0][2])
    def _():
        pl.semaphore_wait(bar, 17)

    @pl.when(seeds[1][2] | seeds[2][2])
    def _():
        pl.semaphore_wait(bar, 16)

    @pl.when(is_root)
    def _():
        pl.semaphore_wait(bar, 18)

    @pl.when(jnp.logical_not(any_relay[0] | any_relay[1] | any_seed | is_root))
    def _():
        pl.semaphore_wait(bar, 4)

    def each_piece(f):
        for r in range(3):
            for q in range(4):
                f(q, r)

    @pl.when(is_root)
    def _():
        each_piece(lambda q, r: [from_root(s, u, q, r).start() for s, u in ((0, 1), (0, 0), (1, 0))])

    for c in copies:
        c.wait()
    relayout_targets(mine, tgt, jnp.bfloat16)
    for s in range(2):
        other = lax.rem(kpt + nk - s, nk)
        make_kern(kern, s, [0.5 * (ks[i, kpt] - ks[i, other]).astype(jnp.float32) + us[s, i].astype(jnp.float32) for i in range(3)])
    acc[...] = jnp.zeros_like(acc)

    for s, u, here in seeds:
        @pl.when(here)
        def _():
            def pass_on(q, r):
                from_root(s, u, q, r).wait_recv()
                from_seed(s, u, q, r).start()
                if s == 0:
                    onward(q, r).start()
            each_piece(pass_on)

    def spread_piece(s, r):
        for d in (2, 1, 3):
            row(s, r, d).start()
        to_twin(s, r, 0, core).start()

    def lead(s):
        for r in range(3):
            @pl.when(relay[s][r])
            def _():
                column(s, r, 1).wait_recv()
                for d in range(1, 8):
                    column(s, r, d).start()
                spread_piece(s, r)

    def rest(s):
        for r in range(3):
            @pl.when(jnp.logical_not(relay[s][r]))
            def _():
                column(s, r, 1).wait_recv()
                spread_piece(s, r)

    def take(s):
        for r in range(3):
            for d in (1, 3, 2):
                arrived(s, r, d).wait_recv()
                to_twin(s, r, d, core).start()

    def finish(s):
        for r in range(3):
            for d in range(4):
                to_twin(s, r, d, 1 - core).wait_recv()

    lead(0)
    rest(0)
    lead(1)
    take(0)

    def one(u, _):
        m = lax.rem(core + u, 2)

        @pl.when(u == 1)
        def _():
            finish(0)

        @pl.when(u == 3)
        def _():
            finish(1)

        phase_a(src.at[u // 2, m], tgt, spr, b, left, right)

        @pl.when(u == 0)
        def _():
            rest(1)

        phase_b(b, cc, kern.at[u // 2], left)

        phase_c(cc, spr, acc, left, right)

        @pl.when(u == 1)
        def _():
            take(1)
        return 0

    lax.fori_loop(0, 4, one, 0)
    gather_out(acc, out, jnp.float32)

    @pl.when(is_root)
    def _():
        each_piece(lambda q, r: [from_root(s, u, q, r).wait_send() for s, u in ((0, 1), (0, 0), (1, 0))])

    @pl.when(any_seed)
    def _():
        each_piece(lambda q, r: from_seed(0, 1, q, r).wait_send())

    @pl.when(seeds[0][2])
    def _():
        each_piece(lambda q, r: onward(q, r).wait_send())

    for s in range(2):
        @pl.when(any_relay[s])
        def _():
            for d in range(1, 8):
                column(s, 0, d).wait_send()
        for r in range(3):
            for d in range(1, 4):
                row(s, r, d).wait_send()
            for d in range(4):
                to_twin(s, r, d, core).wait_send()


def on_device(orbitals, koff, umklapp):
    bf = jnp.bfloat16
    loc = orbitals[0]
    left, right = tables()
    hbm = pl.BlockSpec(memory_space=pl.ANY)
    dma = pltpu.SemaphoreType.DMA
    cube = (2, G * G, L)
    res = pl.pallas_call(
        kernel,
        out_shape=jax.ShapeDtypeStruct(loc.shape, bf),
        in_specs=[hbm] * 5,
        out_specs=pl.BlockSpec(memory_space=pltpu.VMEM),
        scratch_shapes=[pltpu.VMEM((2,) + loc.shape, bf), pltpu.VMEM(cube, bf), pltpu.VMEM(cube, bf)]
        + [pltpu.VMEM(cube, jnp.float32)] * 4
        + [pltpu.VMEM(loc.shape, bf), pltpu.VMEM(left.shape, bf), pltpu.VMEM(right.shape, bf), pltpu.VMEM(loc.shape[1:], bf)]
        + [pltpu.SMEM((3, koff.shape[0]), jnp.int32), pltpu.SMEM(umklapp.shape[1:], jnp.int32)]
        + [dma((5,)), dma((4, 4, 3)), dma((4, 3)), dma((4, 3)), dma((2, 3)), dma((2, 3, 3)), dma((2, 3, 4)), dma((2, 28))],
        compiler_params=pltpu.CompilerParams(collective_id=0, has_side_effects=True, vmem_limit_bytes=56 * 2**20),
    )(loc, koff.T, umklapp[0], jnp.asarray(left), jnp.asarray(right))
    return res[None]


def solution(mesh):
    return jax.shard_map(
        on_device,
        mesh=mesh,
        in_specs=(P("kpt", "band", None, None, None), P(), P("kpt", None, None)),
        out_specs=P("kpt", "band", None, None, None),
        check_vma=False,
    )
```
